128 devices in a mesh: inner: 8 (over x, core), outer: 16 (over z, y).
Axes of the slice: x: 4, y: 4, z: 4, core: 2. Of those that a mesh axis runs over, the one named last changes fastest.
Arguments:
- features: bfloat16 [4096, 16, 512], P(('inner', 'outer')), may hold values from -24 to 24
- cotangent: bfloat16 [4096, 16, 512], P(('inner', 'outer')), may hold values from -6 to 6
- counts: int32 [128], P(('inner', 'outer')), may hold values from 5 to 32, as said below
- senders: int32 [4, 4096], P(None, ('inner', 'outer')), may hold values from 0 to 31, as said below
- angular: float32 [16, 4, 4096], P(None, None, ('inner', 'outer')), may hold values from -5 to 5
- basis: float32 [8, 4, 4096], P(None, None, ('inner', 'outer')), may hold values from -1 to 1
- species: int32 [4096], P(('inner', 'outer')), may hold values from 0 to 88
- w_up: bfloat16 [2, 4, 512, 512], replicated, may hold values from -0.25 to 0.25
- w_first: float32 [2, 8, 64], replicated, may hold values from -2 to 2
- w_second: bfloat16 [2, 64, 2048], replicated, may hold values from -0.75 to 0.75
- w_out: bfloat16 [2, 4, 512, 512], replicated, may hold values from -0.25 to 0.25
- gain: float32 [2, 89, 512], replicated, may hold values from 0.25 to 1.75
Outputs:
- up_grad: float32 [2, 4, 512, 512], P(None, None, ('inner', 'outer'))
- first_grad: float32 [2, 8, 64], replicated
- second_grad: float32 [2, 64, 2048], P(None, None, ('inner', 'outer'))
- out_grad: float32 [2, 4, 512, 512], P(None, None, ('inner', 'outer'))
- gain_grad: float32 [2, 89, 512], P(None, None, ('inner', 'outer'))
- feature_grad: bfloat16 [4096, 16, 512], P(('inner', 'outer'))
The draws below stay inside these ranges and needn't reach their ends.
Inputs may be any that keep to these rules, and one draw needn't show every extreme that they name: `counts`: one device holds exactly 32 live atoms; the others hold between 5 and 16. `senders`: every entry is below the count of the device that holds it.
All inputs are finite; a program needn't handle non-finite values.
Results may differ from the reference program's by a relative error of at most 0.023.
Values sent between devices are 32-bit elements; how exact they have to be, the bound alone decides.
A program may use at most 128 MiB of HBM per device.

```python
import jax
import jax.numpy as jnp
from jax import lax

C = 512
LCOMP = 16
NB = 8
RADH = 64
NSPEC = 89
NEIGH = 4
ATOM_CAP = 32
ATOMS = 4096


def device_counts(key):
    batches = ATOMS // ATOM_CAP
    lower = ATOM_CAP // 6
    upper = ATOM_CAP // 2
    drawn = jax.random.randint(jax.random.fold_in(key, 11), (batches,), lower, upper + 1)
    full = jax.random.randint(jax.random.fold_in(key, 12), (), 0, batches)
    counts = jnp.where(jnp.arange(batches) == full, ATOM_CAP, drawn).astype(jnp.int32)
    return (counts, full)


def draw_counts(key, part):
    counts, full = device_counts(key)
    return counts


def draw_senders(key, part):
    counts, full = device_counts(key)
    key = jax.random.fold_in(key, 5)
    raw = jax.random.randint(key, (NEIGH, ATOMS), 0, 1 << 20)
    owner = jnp.arange(ATOMS) // ATOM_CAP
    local = raw % counts[owner][None, :]
    corner = (jnp.arange(NEIGH)[:, None] == 0) & (jnp.arange(ATOMS)[None, :] == full * ATOM_CAP)
    return jnp.where(corner, ATOM_CAP - 1, local).astype(jnp.int32)


def place_ends(values, rng, least, top_value):
    longest = values.shape.index(max(values.shape))
    spots = []
    for shift in (0, 1):
        where = [jax.random.randint(jax.random.fold_in(rng, axis), (), 0, length) for axis, length in enumerate(values.shape)]
        where[longest] = (where[longest] + shift) % values.shape[longest]
        spots.append(tuple(where))
    return values.at[spots[0]].set(least).at[spots[1]].set(top_value)


def strengthened(values, key, source, target, blocks, factor):
    def block_of(dim):
        return (jnp.arange(values.shape[dim]) // (values.shape[dim] // blocks)).reshape((-1,) + (1,) * (values.ndim - 1 - dim))

    near = jax.random.permutation(key, blocks)[block_of(target)]
    other_side = (block_of(target) + blocks // 2) % blocks
    return jnp.where((block_of(source) == near) | (block_of(source) == other_side), factor * values, values)


def block_scale(key, extent, cuts, least, top_value):
    factor_of, own = 1.0, jax.random.fold_in(key, 6)
    for position, shards_of in cuts:
        heights = jnp.exp(jax.random.uniform(jax.random.fold_in(own, position), (shards_of,), jnp.float32, least / len(cuts), top_value / len(cuts)))
        factor_of = factor_of * jnp.repeat(heights, extent[position] // shards_of).reshape([-1 if axis == position else 1 for axis in range(len(extent))])
    return factor_of


def scatter_about(stream_key, dims, scale, limit, split=(), kind=jnp.bfloat16):
    array = jax.random.normal(stream_key, dims, jnp.float32) * scale
    if len(split) > 0:
        array = block_scale(stream_key, dims, split, -0.22, 0.18) * array
    return jnp.clip(array, min=-limit, max=limit).astype(kind)


def bell_draw_with(rng, extent, scale, most, split, heavy, held_as=jnp.bfloat16):
    values = scale * jax.random.normal(rng, extent, jnp.float32)
    if split:
        values = values * block_scale(rng, extent, split, -0.22, 0.18)
    return jnp.clip(strengthened(values, jax.random.fold_in(rng, 3), *heavy), -most, most).astype(held_as)


def setup_inputs(seed: int = 0) -> dict:
    key_list = jax.random.split(jax.random.key(seed), 13)
    return {
        "features": bell_draw_with(key_list[0], (ATOMS, LCOMP, C), 1.0, 24.0, ((0, 128),), (0, 2, 128, 5.5)),
        "cotangent": scatter_about(key_list[1], (ATOMS, LCOMP, C), 1.0, 6.0, ((0, 128),)),
        "counts": draw_counts(jax.random.fold_in(key_list[12], 71), 0),
        "senders": draw_senders(jax.random.fold_in(key_list[12], 71), 0),
        "angular": scatter_about(key_list[4], (LCOMP, NEIGH, ATOMS), 1.0, 5.0, ((2, 128),), jnp.float32),
        "basis": jnp.clip(jax.random.uniform(key_list[5], (NB, NEIGH, ATOMS), jnp.float32, -1.0, 1.0) * block_scale(key_list[5], (NB, NEIGH, ATOMS), ((2, 128),), -0.4, 0.0), -1.0, 1.0),
        "species": place_ends(jax.random.randint(key_list[6], (ATOMS,), 0, NSPEC), jax.random.fold_in(key_list[6], 1), 0, NSPEC - 1).astype(jnp.int32),
        "w_up": scatter_about(key_list[7], (2, 4, C, C), C ** -0.5, 0.25),
        "w_first": scatter_about(key_list[8], (2, NB, RADH), NB ** -0.5, 2.0, (), jnp.float32),
        "w_second": scatter_about(key_list[9], (2, RADH, 4 * C), RADH ** -0.5, 0.75),
        "w_out": scatter_about(key_list[10], (2, 4, C, C), C ** -0.5, 0.25),
        "gain": jnp.clip(1.0 + 0.15 * jax.random.normal(key_list[11], (2, NSPEC, C), jnp.float32), 0.25, 1.75),
    }


LEVELS = ((0, 1, 0), (1, 4, 1), (4, 9, 2), (9, 16, 3))
CLIP_NORM = 2048.0

def mix(values, weight):
    rows = values.shape[0]
    width = values.shape[2]
    pieces = []
    for first, last, order in LEVELS:
        block = values[:, first:last, :].reshape(rows * (last - first), width)
        pieces.append(jnp.dot(block, weight[order], preferred_element_type=jnp.float32).reshape(rows, last - first, weight.shape[2]))
    return jnp.concatenate(pieces, axis=1)

def expand(radial):
    return jnp.concatenate([jnp.repeat(radial[:, order:order + 1, :], last - first, axis=1) for first, last, order in LEVELS], axis=1)

def interaction(feats, w_up, w_first, w_second, w_out, gain, senders, angular, basis, onehot):
    rows = feats.shape[0]
    width = feats.shape[2]
    slots = senders.shape[0]
    lifted = mix(feats, w_up).astype(jnp.bfloat16)
    flat_basis = jnp.transpose(basis, (1, 2, 0)).reshape(slots * rows, basis.shape[0])
    hidden = jax.nn.silu(jnp.dot(flat_basis, w_first, precision=lax.Precision.HIGHEST)).astype(jnp.bfloat16)
    radial = jnp.dot(hidden, w_second, preferred_element_type=jnp.float32).reshape(slots, rows, 4, width)
    angular_t = jnp.transpose(angular, (1, 2, 0))

    def slot_step(total, inputs):
        index, weights, harmonics = inputs
        source = jnp.take(lifted, index, axis=0).astype(jnp.float32)
        message = expand(weights) * (harmonics[:, :, None] * source[:, 0:1, :] + source)
        return (total + message, None)
    total, unused = lax.scan(jax.checkpoint(slot_step), jnp.zeros((rows, feats.shape[1], width), jnp.float32), (senders, radial, angular_t))
    summed = (total / slots).astype(jnp.bfloat16)
    mixed = mix(summed, w_out)
    scalar = mixed[:, 0, :]
    gates = jax.nn.sigmoid(scalar)
    skip_gain = jnp.dot(onehot, gain, precision=lax.Precision.HIGHEST)
    result = jnp.concatenate([jax.nn.silu(scalar)[:, None, :], mixed[:, 1:, :] * gates[:, None, :]], axis=1)
    return result + skip_gain[:, None, :] * feats.astype(jnp.float32)

def device_grads(params, feats, cot, count, senders, angular, basis, species):
    rows = feats.shape[0]
    onehot = (species[:, None] == jnp.arange(params[4].shape[1], dtype=jnp.int32)[None, :]).astype(jnp.float32)
    live = (jnp.arange(rows, dtype=jnp.int32) < count).astype(jnp.float32)

    def loss_of(weights, inputs):
        w_up, w_first, w_second, w_out, gain = weights
        first = interaction(inputs, w_up[0], w_first[0], w_second[0], w_out[0], gain[0], senders, angular, basis, onehot).astype(jnp.bfloat16)
        second = interaction(first, w_up[1], w_first[1], w_second[1], w_out[1], gain[1], senders, angular, basis, onehot)
        return jnp.sum(second * cot.astype(jnp.float32) * live[:, None, None])
    loss, pullback = jax.vjp(loss_of, params, feats)
    weight_grads, feat_grad = pullback(jnp.ones((), jnp.float32))
    return (tuple((g.astype(jnp.float32) for g in weight_grads)), feat_grad)

def reference(features, cotangent, counts, senders, angular, basis, species, w_up, w_first, w_second, w_out, gain):
    batches = counts.shape[0]
    cap = features.shape[0] // batches
    params = (w_up, w_first, w_second, w_out, gain)
    feats_b = features.reshape(batches, cap, features.shape[1], features.shape[2])
    cot_b = cotangent.reshape(batches, cap, features.shape[1], features.shape[2])
    send_b = jnp.transpose(senders.reshape(senders.shape[0], batches, cap), (1, 0, 2))
    ang_b = jnp.transpose(angular.reshape(angular.shape[0], angular.shape[1], batches, cap), (2, 0, 1, 3))
    basis_b = jnp.transpose(basis.reshape(basis.shape[0], basis.shape[1], batches, cap), (2, 0, 1, 3))
    spec_b = species.reshape(batches, cap)

    def batch_step(totals, inputs):
        feats, cot, count, send, ang, bas, spec = inputs
        grads, feat_grad = device_grads(params, feats, cot, count, send, ang, bas, spec)
        return (tuple((t + g for t, g in zip(totals, grads))), feat_grad)
    start = tuple((jnp.zeros(p.shape, jnp.float32) for p in params))
    totals, feat_grads = lax.scan(batch_step, start, (feats_b, cot_b, counts, send_b, ang_b, basis_b, spec_b))
    squares = sum((jnp.sum(t * t) for t in totals))
    scale = jnp.minimum(1.0, CLIP_NORM / jnp.sqrt(squares + 1e-06))
    up_grad, first_grad, second_grad, out_grad, gain_grad = tuple((t * scale for t in totals))
    return (up_grad, first_grad, second_grad, out_grad, gain_grad, feat_grads.reshape(features.shape))
```

```python
import functools

import jax
import jax.numpy as jnp
from jax import lax
from jax.experimental import pallas as pl
from jax.experimental.pallas import tpu as pltpu
from jax.sharding import PartitionSpec as P

MESH = pl.DeviceIdType.MESH
F32, BF16, I32 = jnp.float32, jnp.bfloat16, jnp.int32
HIGH = lax.Precision.HIGHEST
CLIP_NORM = 2048.0

LEVELS = ((0, 1), (1, 4), (4, 9), (9, 16))
ATOMS = 32
EDGES = 128
C = 512

MATS = (
    [("out", 1, d) for d in range(4)]
    + [("up", 1, d) for d in range(4)]
    + [("out", 0, d) for d in range(4)]
    + [("up", 0, d) for d in range(4)]
)
CLASS = [q % 3 for q in range(16)]
CLASS[14] = 1
SEC, GAIN = 16, 17
CLASS = CLASS + [2, 2]
NUNITS = 18
ORDER = ((2, 0, 1), (1, 2, 0), (0, 1, 2))
PAIRS = []
for _k in range(3):
    _own = [q for q in range(16) if CLASS[q] == _k]
    PAIRS += [(_own[n], _own[n + 1]) for n in range(0, len(_own), 2)]
NPAIRS = len(PAIRS)
D1, D2, D3 = 3, 6, 9
OUT_SLOTS = 4


def dot(a, b, precision=None):
    return lax.dot_general(
        a, b, (((1,), (0,)), ((), ())), precision=precision, preferred_element_type=F32
    )


def dot_nt(a, b, precision=None):
    return lax.dot_general(
        a, b, (((1,), (1,)), ((), ())), precision=precision, preferred_element_type=F32
    )


def position():
    inner, outer = lax.axis_index("inner"), lax.axis_index("outer")
    return inner // 2, inner % 2, outer // 4, outer % 4


def peer(axis, step):
    x, c, z, y = position()
    if axis == 0:
        x = (x + step) % 4
    elif axis == 1:
        z = (z + step) % 4
    elif axis == 2:
        y = (y + step) % 4
    else:
        c = 1 - c
    return (x * 2 + c, z * 4 + y)


def along(axis):
    x, c, z, y = position()
    return (x, z, y, c)[axis]


def rows_of(first, last):
    return slice(first * ATOMS, last * ATOMS)


def iota(shape, dim):
    return lax.broadcasted_iota(I32, shape, dim)


def onehot(mask):
    return jnp.where(mask, 1.0, 0.0).astype(BF16)


def kernel(
    counts, feat, cot, send, ang, basis, spec, w_first, gain, wup_h, wsec_h, wout_h,
    up_o, first_o, sec_o, out_o, gain_o, fg_o,
    wup, wout, wsec, wfp, gpad, wsem,
    xb, lg, rad, pre, hid, sm, mx, grow, abc, lbuf, dyb, dmx, dsb, dr, dl0, dsrc, dl, drt, xt, pt, dsk,
    own, own_s, own_g, outb, outb_s, outb_g,
    rx0, rx0_s, rx0_g, rx1, rx1_s, rx1_g, rx2, rx2_s, rx2_g,
    f2, f2_s, f2_g, s3, s3_s, s3_g, rx3, rx3_s, rx3_g, fin, fin_s, fin_g,
    red, redrx,
    ss0, rs0, ss1, rs1, ss2, rs2, ss3, rs3, ssr, rsr,
):
    x, c, z, y = position()

    loads = {}
    for layer in (0, 1):
        loads["up", layer] = pltpu.make_async_copy(wup_h.at[layer], wup.at[layer], wsem.at[3 * layer])
        loads["sec", layer] = pltpu.make_async_copy(
            wsec_h.at[layer], wsec.at[layer, pl.ds(64 * layer, 64)], wsem.at[3 * layer + 1]
        )
        loads["out", layer] = pltpu.make_async_copy(wout_h.at[layer], wout.at[layer], wsem.at[3 * layer + 2])
    for layer in (0, 1):
        for name in ("up", "sec", "out"):
            loads[name, layer].start()

    barrier = pltpu.get_barrier_semaphore()
    for axis in range(3):
        for step in (1, 2, 3):
            pl.semaphore_signal(barrier, inc=1, device_id=peer(axis, step), device_id_type=MESH)
    pl.semaphore_signal(barrier, inc=1, device_id=peer(3, 1), device_id_type=MESH)

    count = counts[0]
    r, cl = iota((C, C), 0), iota((C, C), 1)
    to_comp = onehot(cl == (r & 31) * 16 + (r >> 5))
    xb[0] = dot(to_comp, feat[...]).astype(BF16)
    to_comp_live = onehot((cl == (r & 31) * 16 + (r >> 5)) & ((r & 31) < count))
    dyb[...] = dot(to_comp_live, cot[...])
    for k in range(3):
        digits = ((r >> 6) & 3, (r >> 4) & 3, (r >> 2) & 3)
        held = {ORDER[k][n]: digits[n] for n in range(3)}
        source = held[0] * 128 + ((r >> 8) ^ c) * 64 + held[1] * 16 + held[2] * 4 + (r & 3)
        pt[k] = onehot(cl == source)
    eye = onehot(r == cl)
    pt[3] = eye
    eye_e = onehot(iota((EDGES, EDGES), 0) == iota((EDGES, EDGES), 1))
    row = jnp.concatenate([send[s : s + 1, :] for s in range(4)], axis=1)
    scatter = onehot(iota((ATOMS, EDGES), 0) == row)
    gather = dot_nt(eye_e, scatter).astype(BF16)
    ang2 = jnp.concatenate([ang[:, s, :] for s in range(4)], axis=1)
    basis2 = jnp.concatenate([basis[:, s, :] for s in range(4)], axis=1)
    ang_t = jnp.transpose(ang2)
    for m in range(16):
        abc[m] = jnp.broadcast_to(ang_t[:, m : m + 1], (EDGES, 128))
    basis_t = jnp.transpose(basis2)
    kind_t = onehot(iota((128, ATOMS), 0) == spec[...])
    eye_a = onehot(iota((ATOMS, ATOMS), 0) == iota((ATOMS, ATOMS), 1))
    kind = dot_nt(eye_a, kind_t)
    kind_b = kind.astype(BF16)
    wfp[...] = jnp.zeros_like(wfp)
    gpad[...] = jnp.zeros_like(gpad)
    for layer in (0, 1):
        wfp[layer, :, 64 * layer : 64 * layer + 64] = w_first[layer]
        gpad[layer, 0:89, :] = gain[layer]
        wsec[layer, 64 * (1 - layer) : 64 * (1 - layer) + 64, :] = jnp.zeros((64, 2048), BF16)
        grow[layer] = dot(kind, gpad[layer], HIGH)

    tiles = [(s, t) for t in range(4) for s in range(4)]

    def edge_rows(s):
        return pl.ds(s * ATOMS, ATOMS)

    def lanes(t):
        return pl.ds(t * 128, 128)

    for layer in (0, 1):
        loads["up", layer].wait()
        for d, (a, b) in enumerate(LEVELS):
            lbuf[rows_of(a, b), :] = dot(xb[layer, rows_of(a, b), :], wup[layer, d]).astype(BF16)
        loads["sec", layer].wait()
        p = dot(basis_t, wfp[layer], HIGH)
        pre[layer] = p
        hid[layer] = (p * jax.nn.sigmoid(p)).astype(BF16)
        for d in range(4):
            rad[layer, :, d * C : (d + 1) * C] = dot(hid[layer], wsec[layer, :, d * C : (d + 1) * C])

        for d, (a, b) in enumerate(LEVELS):

            def message(m, carry, d=d, layer=layer):
                at = pl.multiple_of(m * ATOMS, ATOMS)
                lg[layer, m] = dot(gather, lbuf[pl.ds(at, ATOMS), :]).astype(BF16)
                for t in range(4):
                    total = jnp.zeros((ATOMS, 128), F32)
                    for s in range(4):
                        src = lg[layer, m, edge_rows(s), lanes(t)].astype(F32)
                        src0 = lg[layer, 0, edge_rows(s), lanes(t)].astype(F32)
                        weight = rad[layer, edge_rows(s), pl.ds(d * C + t * 128, 128)]
                        total += weight * (abc[m, edge_rows(s), :] * src0 + src)
                    sm[layer, pl.ds(at, ATOMS), lanes(t)] = (total * 0.25).astype(BF16)
                return carry

            lax.fori_loop(a, b, message, 0)
        loads["out", layer].wait()
        for d, (a, b) in enumerate(LEVELS):
            mx[layer, rows_of(a, b), :] = dot(sm[layer, rows_of(a, b), :], wout[layer, d])
        if layer == 0:

            def gated(m, carry):
                at = pl.multiple_of(m * ATOMS, ATOMS)
                gate = jax.nn.sigmoid(mx[0, 0:ATOMS, :])
                value = mx[0, pl.ds(at, ATOMS), :] * gate
                value += grow[0] * xb[0, pl.ds(at, ATOMS), :].astype(F32)
                xb[1, pl.ds(at, ATOMS), :] = value.astype(BF16)
                return carry

            lax.fori_loop(0, 16, gated, 0)

    def bufs(u):
        if u == SEC:
            return own_s, outb_s, rx0_s, rx1_s, rx2_s, f2_s, 1024
        if u == GAIN:
            return own_g, outb_g, rx0_g, rx1_g, rx2_g, f2_g, 256
        return own.at[u], outb.at[u % OUT_SLOTS], rx0.at[u], rx1.at[u], rx2.at[u], f2.at[u], 256

    def step0(u):
        _, out_r, r0, _, _, _, _ = bufs(u)
        return pltpu.make_async_remote_copy(
            src_ref=out_r, dst_ref=r0, send_sem=ss0.at[u], recv_sem=rs0.at[u],
            device_id=peer(3, 1), device_id_type=MESH,
        )

    def chunk(ref, rows, which, part, parts):
        size = rows // 4 // parts
        return ref.at[pl.ds(pl.multiple_of(which * (rows // 4) + part * size, size), size)]

    def step1(u):
        o, _, _, r1, _, _, rows = bufs(u)
        axis = ORDER[CLASS[u]][0]
        p = along(axis)
        plan = (
            ((p + 2) % 4, 0, 1), ((p + 1) % 4, 1, 1),
            ((p + 2) % 4, 1, 3), ((p + 3) % 4, 0, 3),
            ((p + 1) % 4, 0, 1), ((p + 3) % 4, 1, 3),
        )
        return [
            pltpu.make_async_remote_copy(
                src_ref=chunk(o, rows, which, part, 2), dst_ref=r1.at[n],
                send_sem=ss1.at[6 * u + n], recv_sem=rs1.at[6 * u + n],
                device_id=peer(axis, way), device_id_type=MESH,
            )
            for n, (which, part, way) in enumerate(plan)
        ]

    def step2(u):
        o, _, _, _, r2, _, rows = bufs(u)
        first, second, _ = ORDER[CLASS[u]]
        p1, p2 = along(first), along(second)
        size = rows // 16
        return [
            pltpu.make_async_remote_copy(
                src_ref=o.at[pl.ds(pl.multiple_of(p1 * (rows // 4) + ((p2 + j) % 4) * size, size), size)],
                dst_ref=r2.at[j - 1],
                send_sem=ss2.at[3 * u + j - 1], recv_sem=rs2.at[3 * u + j - 1],
                device_id=peer(second, j), device_id_type=MESH,
            )
            for j in (1, 2, 3)
        ]

    def step3(n):
        if n < NPAIRS:
            k, src, dst = CLASS[PAIRS[n][0]], s3.at[n], rx3.at[n]
        elif n == NPAIRS:
            k, src, dst = 2, s3_s, rx3_s
        else:
            k, src, dst = 2, s3_g, rx3_g
        axis = ORDER[k][2]
        p = along(axis)
        return [
            pltpu.make_async_remote_copy(
                src_ref=src.at[(p + j) % 4], dst_ref=dst.at[j - 1],
                send_sem=ss3.at[3 * n + j - 1], recv_sem=rs3.at[3 * n + j - 1],
                device_id=peer(axis, j), device_id_type=MESH,
            )
            for j in (1, 2, 3)
        ]

    sent = []

    def start(copies):
        for one in copies:
            one.start()
            sent.append(one)

    done2 = set()

    def service(tick):
        u = tick
        if u < NUNITS:
            start([step0(u)])
        u = tick - 1
        if 0 <= u < NUNITS:
            o, _, r0, _, _, _, rows = bufs(u)
            step0(u).wait_recv()
            o[...] = o[...] + r0[...]
            start(step1(u)[:4])
        u = tick - D1
        if 0 <= u < NUNITS:
            o, _, _, r1, _, _, rows = bufs(u)
            copies = step1(u)
            p = along(ORDER[CLASS[u]][0])
            for first, second, which, part in ((0, 4, (p + 1) % 4, 0), (2, 5, (p + 3) % 4, 1)):
                copies[first].wait_recv()
                view = chunk(o, rows, which, part, 2)
                view[...] = view[...] + r1[first]
                start([copies[second]])
        u = tick - D2
        if 0 <= u < NUNITS:
            o, _, _, r1, _, _, rows = bufs(u)
            copies = step1(u)
            p = along(ORDER[CLASS[u]][0])
            for direct, summed, part in ((3, 4, 0), (1, 5, 1)):
                copies[direct].wait_recv()
                copies[summed].wait_recv()
                view = chunk(o, rows, p, part, 2)
                view[...] = view[...] + r1[direct] + r1[summed]
            start(step2(u))
        u = tick - D3
        if 0 <= u < NUNITS:
            o, _, _, _, r2, ff, rows = bufs(u)
            first, second, _ = ORDER[CLASS[u]]
            for copy in step2(u):
                copy.wait_recv()
            size = rows // 16
            at = pl.multiple_of(along(first) * (rows // 4) + along(second) * size, size)
            value = o[pl.ds(at, size)] + r2[0] + r2[1] + r2[2]
            if u == SEC:
                for n in range(4):
                    s3_s[n] = value[16 * n : 16 * n + 16]
                start(step3(NPAIRS))
            elif u == GAIN:
                for n in range(4):
                    s3_g[n] = jnp.concatenate(
                        [value[4 * n : 4 * n + 4, 0:128], value[4 * n : 4 * n + 4, 128:256]], axis=0
                    )
                start(step3(NPAIRS + 1))
            else:
                ff[...] = value
                done2.add(u)
                for n, (ua, ub) in enumerate(PAIRS):
                    if u in (ua, ub) and ua in done2 and ub in done2:
                        va, vb = f2[ua], f2[ub]
                        for q in range(4):
                            s3[n, q] = jnp.concatenate([va[4 * q : 4 * q + 4], vb[4 * q : 4 * q + 4]], axis=0)
                        start(step3(n))

    def put(u, a, g):
        rows = a.shape[0]
        xt[:, 0:rows] = dot_nt(pt[CLASS[u]], a).astype(BF16)
        if u >= OUT_SLOTS:
            step0(u - OUT_SLOTS).wait_send()
        o, out_r = bufs(u)[:2]
        o[...] = dot(xt[0:256, 0:rows], g)
        out_r[...] = dot(xt[256:512, 0:rows], g)

    waited_barrier = False
    tick = 0
    for layer in (1, 0):
        t = mx[layer, 0:ATOMS, :]
        gate = jax.nn.sigmoid(t)
        dy0 = dyb[0:ATOMS, :]

        def gates(m, carry, layer=layer, gate=gate):
            dgate, dskip = carry
            at = pl.ds(pl.multiple_of(m * ATOMS, ATOMS), ATOMS)
            dy = dyb[at, :]
            dmx[at, :] = (dy * gate).astype(BF16)
            dgate += dy * mx[layer, at, :]
            dskip += dy * xb[layer, at, :].astype(F32)
            return dgate, dskip

        zero = jnp.zeros((ATOMS, C), F32)
        dgate, dskip = lax.fori_loop(
            1, 16, gates, (zero, dy0 * xb[layer, 0:ATOMS, :].astype(F32))
        )
        slope = gate * (1.0 - gate)
        dmx[0:ATOMS, :] = (dy0 * (gate + t * slope) + dgate * slope).astype(BF16)
        dsk[layer] = dskip

        if not waited_barrier:
            pl.semaphore_wait(barrier, 10)
            waited_barrier = True
        for d, (a, b) in enumerate(LEVELS):
            put(tick, sm[layer, rows_of(a, b), :], dmx[rows_of(a, b), :])
            service(tick)
            tick += 1
        for d, (a, b) in enumerate(LEVELS):
            dsb[rows_of(a, b), :] = dot_nt(dmx[rows_of(a, b), :], wout[layer, d]) * 0.25

        dr[...] = jnp.zeros_like(dr)
        dl0[...] = jnp.zeros_like(dl0)
        for d, (a, b) in enumerate(LEVELS):

            def back(m, carry, d=d, layer=layer, lone=(d == 0)):
                at = pl.multiple_of(m * ATOMS, ATOMS)
                for t in range(4):
                    dt = dsb[pl.ds(at, ATOMS), lanes(t)]
                    for s in range(4):
                        src = lg[layer, m, edge_rows(s), lanes(t)].astype(F32)
                        src0 = lg[layer, 0, edge_rows(s), lanes(t)].astype(F32)
                        wide = pl.ds(d * C + t * 128, 128)
                        weight = rad[layer, edge_rows(s), wide]
                        harm = abc[m, edge_rows(s), :]
                        q = dt * weight
                        dr[edge_rows(s), wide] += dt * (harm * src0 + src)
                        if lone:
                            dl0[edge_rows(s), lanes(t)] += q + harm * q
                        else:
                            dl0[edge_rows(s), lanes(t)] += harm * q
                            dsrc[edge_rows(s), lanes(t)] = q.astype(BF16)
                if not lone:
                    dl[pl.ds(at, ATOMS), :] = dot(scatter, dsrc[...]).astype(BF16)
                return carry

            if d == 0:
                back(0, 0)
            else:
                lax.fori_loop(a, b, back, 0)
        dl[0:ATOMS, :] = dot(scatter, dl0[...].astype(BF16)).astype(BF16)

        for d, (a, b) in enumerate(LEVELS):
            put(tick, xb[layer, rows_of(a, b), :], dl[rows_of(a, b), :])
            service(tick)
            tick += 1
        for d, (a, b) in enumerate(LEVELS):
            dsb[rows_of(a, b), :] = dot_nt(dl[rows_of(a, b), :], wup[layer, d])

        def skip(m, carry, layer=layer):
            at = pl.ds(pl.multiple_of(m * ATOMS, ATOMS), ATOMS)
            dyb[at, :] = dsb[at, :] + grow[layer] * dyb[at, :]
            return carry

        lax.fori_loop(0, 16, skip, 0)
        drb = dr[...].astype(BF16)
        for d in range(4):
            drt[layer, d] = dot_nt(pt[3], drb[:, d * C : (d + 1) * C]).astype(BF16)
        dhid = dot_nt(drb, wsec[layer])
        p = pre[layer]
        sg = jax.nn.sigmoid(p)
        dpre = dhid * (sg * (1.0 + p * (1.0 - sg)))
        term = dot(basis2, dpre, HIGH)
        if layer == 1:
            red[0] = term
        else:
            red[0] = red[0] + term

    for d in range(4):
        blk = dot(drt[0, d], hid[0]) + dot(drt[1, d], hid[1])
        for half in range(2):
            part = blk[256 * half : 256 * half + 256]
            @pl.when(c == half)
            def _(part=part, d=d):
                own_s[256 * d : 256 * d + 256, :] = part

            @pl.when(c != half)
            def _(part=part, d=d):
                outb_s[256 * d : 256 * d + 256, :] = part

    service(tick)
    tick += 1
    for layer in (0, 1):
        hi = dsk[layer].astype(BF16)
        lo = (dsk[layer] - hi.astype(F32)).astype(BF16)
        blk = dot(dot_nt(pt[2], hi).astype(BF16), kind_b) + dot(dot_nt(pt[2], lo).astype(BF16), kind_b)
        own_g[:, 128 * layer : 128 * layer + 128] = blk[0:256]
        outb_g[:, 128 * layer : 128 * layer + 128] = blk[256:512]
    service(tick)
    tick += 1

    to_atom = onehot(cl == (r & 15) * 32 + (r >> 4))
    fg_o[...] = dot(to_atom, dyb[...].astype(BF16)).astype(BF16)

    def all_sum(which, stage):
        axis = stage
        n = 2 if axis == 3 else 4
        p = along(axis)
        base = (which * 4 + stage) * 4
        copies = [
            pltpu.make_async_remote_copy(
                src_ref=red.at[which * 5 + stage], dst_ref=redrx.at[base + p],
                send_sem=ssr.at[base + j], recv_sem=rsr.at[base + p],
                device_id=peer(axis, j), device_id_type=MESH,
            )
            for j in range(1, n)
        ]
        waits = [
            pltpu.make_async_remote_copy(
                src_ref=red.at[which * 5 + stage], dst_ref=redrx.at[base + (p + j) % n],
                send_sem=ssr.at[base + j], recv_sem=rsr.at[base + (p + j) % n],
                device_id=peer(axis, j), device_id_type=MESH,
            )
            for j in range(1, n)
        ]
        return copies, waits, base, n, p

    def all_sum_start(which, stage):
        copies, _, base, n, p = all_sum(which, stage)
        start(copies)
        redrx[base + p] = red[which * 5 + stage]

    def all_sum_end(which, stage):
        _, waits, base, n, p = all_sum(which, stage)
        for one in waits:
            one.wait_recv()
        value = redrx[base]
        for j in range(1, n):
            value = value + redrx[base + j]
        red[which * 5 + stage + 1] = value

    all_sum_start(0, 0)
    stage = 0
    while tick < NUNITS + D3:
        service(tick)
        tick += 1
        if stage < 4 and tick % 2 == 0:
            all_sum_end(0, stage)
            stage += 1
            if stage < 4:
                all_sum_start(0, stage)

    squares = jnp.zeros((8, 128), F32)
    for n in range(NPAIRS + 2):
        if n < NPAIRS:
            src, rec, out, k = s3.at[n], rx3.at[n], fin.at[n], CLASS[PAIRS[n][0]]
        elif n == NPAIRS:
            src, rec, out, k = s3_s, rx3_s, fin_s, 2
        else:
            src, rec, out, k = s3_g, rx3_g, fin_g, 2
        for copy in step3(n):
            copy.wait_recv()
        value = src[along(ORDER[k][2])] + rec[0] + rec[1] + rec[2]
        out[...] = value
        sq = value * value
        if n < NPAIRS:
            for q in range(4):
                squares += sq[:, 128 * q : 128 * q + 128]
        elif n == NPAIRS:
            squares += sq[0:8] + sq[8:16]
        else:
            squares += sq
    red[5] = squares
    for stage in range(4):
        all_sum_start(1, stage)
        all_sum_end(1, stage)
    first_sum = red[4]
    total = jnp.sum(jnp.sum(red[9] + first_sum * first_sum, axis=1, keepdims=True), axis=0, keepdims=True)
    scale = jnp.minimum(1.0, CLIP_NORM / jnp.sqrt(total + 1e-6))

    for n, pair in enumerate(PAIRS):
        value = fin[n] * scale
        for half, u in enumerate(pair):
            which, layer, d = MATS[u]
            ref = up_o if which == "up" else out_o
            ref[layer, d] = value[4 * half : 4 * half + 4]
    scaled = first_sum * scale
    first_o[0] = scaled[:, 0:64]
    first_o[1] = scaled[:, 64:128]
    sec_t = jnp.transpose(fin_s[...] * scale)
    sec_o[0] = sec_t[0:64]
    sec_o[1] = sec_t[64:128]
    gain_t = jnp.transpose(fin_g[...] * scale)
    gain_o[0] = gain_t[0:89, 0:4]
    gain_o[1] = gain_t[0:89, 4:8]

    waited = set(range(0, NUNITS))
    for one in sent:
        pass
    for u in range(NUNITS):
        if not (u < 16 and u + OUT_SLOTS < 16):
            step0(u).wait_send()
        for copy in step1(u) + step2(u):
            copy.wait_send()
    for n in range(NPAIRS + 2):
        for copy in step3(n):
            copy.wait_send()
    for which in range(2):
        for stage in range(4):
            for copy in all_sum(which, stage)[0]:
                copy.wait_send()


def per_device(features, cotangent, counts, senders, angular, basis, species, w_up, w_first, w_second, w_out, gain):
    vm, hbm = pl.BlockSpec(memory_space=pltpu.VMEM), pl.BlockSpec(memory_space=pl.ANY)
    V = pltpu.VMEM
    dma = pltpu.SemaphoreType.DMA
    scratch = [
        V((2, 4, C, C), BF16), V((2, 4, C, C), BF16), V((2, 128, 2048), BF16), V((2, 8, 128), F32), V((2, 128, C), F32), dma((6,)),
        V((2, C, C), BF16),
        V((2, 16, EDGES, C), BF16),
        V((2, EDGES, 2048), F32),
        V((2, EDGES, 128), F32),
        V((2, EDGES, 128), BF16),
        V((2, C, C), BF16),
        V((2, C, C), F32),
        V((2, ATOMS, C), F32),
        V((16, EDGES, 128), F32),
        V((C, C), BF16),
        V((C, C), F32),
        V((C, C), BF16),
        V((C, C), F32),
        V((EDGES, 2048), F32),
        V((EDGES, C), F32),
        V((EDGES, C), BF16),
        V((C, C), BF16),
        V((2, 4, C, EDGES), BF16),
        V((C, 256), BF16),
        V((4, C, C), BF16),
        V((2, ATOMS, C), F32),
        V((16, 256, C), F32), V((1024, 128), F32), V((256, 256), F32),
        V((OUT_SLOTS, 256, C), F32), V((1024, 128), F32), V((256, 256), F32),
        V((16, 256, C), F32), V((1024, 128), F32), V((256, 256), F32),
        V((16, 6, 32, C), F32), V((6, 128, 128), F32), V((6, 32, 256), F32),
        V((16, 3, 16, C), F32), V((3, 64, 128), F32), V((3, 16, 256), F32),
        V((16, 16, C), F32), V((64, 128), F32), V((16, 256), F32),
        V((NPAIRS, 4, 8, C), F32), V((4, 16, 128), F32), V((4, 8, 128), F32),
        V((NPAIRS, 3, 8, C), F32), V((3, 16, 128), F32), V((3, 8, 128), F32),
        V((NPAIRS, 8, C), F32), V((16, 128), F32), V((8, 128), F32),
        V((10, 8, 128), F32), V((32, 8, 128), F32),
        dma((NUNITS,)), dma((NUNITS,)), dma((6 * NUNITS,)), dma((6 * NUNITS,)),
        dma((3 * NUNITS,)), dma((3 * NUNITS,)), dma((3 * (NPAIRS + 2),)), dma((3 * (NPAIRS + 2),)),
        dma((32,)), dma((32,)),
    ]
    shape = jax.ShapeDtypeStruct
    up, first, second, out, gain_grad, feature_grad = pl.pallas_call(
        kernel,
        name="interaction_grads",
        out_shape=(
            shape((2, 4, 4, C), F32), shape((2, 8, 64), F32), shape((2, 64, 16), F32),
            shape((2, 4, 4, C), F32), shape((2, 89, 4), F32), shape((C, C), BF16),
        ),
        in_specs=[pl.BlockSpec(memory_space=pltpu.SMEM)] + [vm] * 8 + [hbm] * 3,
        out_specs=(vm,) * 6,
        scratch_shapes=scratch,
        compiler_params=pltpu.CompilerParams(
            collective_id=0, has_side_effects=True, vmem_limit_bytes=63 * 2**20
        ),
        cost_estimate=pl.CostEstimate(flops=8 * 10**9, bytes_accessed=12 * 10**6, transcendentals=10**5),
    )(
        counts, features.reshape(C, C), cotangent.reshape(C, C), senders, angular, basis,
        species.reshape(1, ATOMS), w_first, gain, w_up, w_second, w_out,
    )
    return up, first, second, out, gain_grad, feature_grad.reshape(features.shape)


def solution(mesh):
    both = ("inner", "outer")
    return jax.shard_map(
        per_device,
        mesh=mesh,
        in_specs=(
            P(both, None, None), P(both, None, None), P(both), P(None, both), P(None, None, both),
            P(None, None, both), P(both), P(), P(), P(), P(), P(),
        ),
        out_specs=(
            P(None, None, both, None), P(), P(None, None, both), P(None, None, both, None),
            P(None, None, both), P(both, None, None),
        ),
        check_vma=False,
    )
```

```python
import functools

import jax
import jax.numpy as jnp
from jax import lax
from jax.experimental import pallas as pl
from jax.experimental.pallas import tpu as pltpu
from jax.sharding import PartitionSpec as P

MESH = pl.DeviceIdType.MESH
F32, BF16, I32 = jnp.float32, jnp.bfloat16, jnp.int32
HIGH = lax.Precision.HIGHEST
CLIP_NORM = 2048.0

LEVELS = ((0, 1), (1, 4), (4, 9), (9, 16))
ATOMS = 32
EDGES = 128
C = 512

MATS = (
    [("out", 1, d) for d in range(4)]
    + [("up", 1, d) for d in range(4)]
    + [("out", 0, d) for d in range(4)]
    + [("up", 0, d) for d in range(4)]
)
CLASS = [q % 3 for q in range(16)]
CLASS[14] = 1
SEC, GAIN = 16, 17
CLASS = CLASS + [2, 2]
NUNITS = 18
ORDER = ((2, 0, 1), (1, 2, 0), (0, 1, 2))
PAIRS = []
for _k in range(3):
    _own = [q for q in range(16) if CLASS[q] == _k]
    PAIRS += [(_own[n], _own[n + 1]) for n in range(0, len(_own), 2)]
NPAIRS = len(PAIRS)
D0, D1, D2, D3 = 2, 6, 10, 13
OUT_SLOTS = 4


def dot(a, b, precision=None):
    return lax.dot_general(
        a, b, (((1,), (0,)), ((), ())), precision=precision, preferred_element_type=F32
    )


def dot_nt(a, b, precision=None):
    return lax.dot_general(
        a, b, (((1,), (1,)), ((), ())), precision=precision, preferred_element_type=F32
    )


GROUPS = ((0, 8), (1, 16))


def position():
    inner, outer = lax.axis_index("inner"), lax.axis_index("outer")
    return inner // 2, inner % 2, outer // 4, outer % 4


def peer(axis, step):
    x, c, z, y = position()
    if axis == 0:
        x = (x + step) % 4
    elif axis == 1:
        z = (z + step) % 4
    elif axis == 2:
        y = (y + step) % 4
    else:
        c = 1 - c
    return (x * 2 + c, z * 4 + y)


def group_peer(stage, step):
    inner, outer = lax.axis_index("inner"), lax.axis_index("outer")
    if stage == 0:
        return ((inner + step) % 8, outer)
    return (inner, (outer + step) % 16)


def along(axis):
    x, c, z, y = position()
    return (x, z, y, c)[axis]


def rows_of(first, last):
    return slice(first * ATOMS, last * ATOMS)


def iota(shape, dim):
    return lax.broadcasted_iota(I32, shape, dim)


def onehot(mask):
    return jnp.where(mask, 1.0, 0.0).astype(BF16)


def kernel(
    counts, send, ang, basis, spec, w_first, feat_h, cot_h, gain_h, wup_h, wsec_h, wout_h,
    fin, fin_s, fin_g, sums, fg_o,
    feat, cot, gain, wup, wout, wsec, wfp, gpad, wsem,
    xb, lg, rad, pre, hid, sm, mx, grow, abc, lbuf, dyb, dmx, dsb, dr, dl, drt, xt, pt, dsk, fgb,
    own, own_s, own_g, outb, outb_s, outb_g,
    rx0, rx0_s, rx0_g, rx1, rx1_s, rx1_g, rx2, rx2_s, rx2_g,
    f2, f2_s, f2_g, s3, s3_s, s3_g, rx3, rx3_s, rx3_g,
    red, redrx,
    ss0, rs0, ss1, rs1, ss2, rs2, ss3, rs3, ssr, rsr,
):
    x, c, z, y = position()

    loads = {}
    for layer in (0, 1):
        loads["up", layer] = pltpu.make_async_copy(wup_h.at[layer], wup.at[layer], wsem.at[3 * layer])
        loads["sec", layer] = pltpu.make_async_copy(
            wsec_h.at[layer], wsec.at[layer, pl.ds(64 * layer, 64)], wsem.at[3 * layer + 1]
        )
        loads["out", layer] = pltpu.make_async_copy(wout_h.at[layer], wout.at[layer], wsem.at[3 * layer + 2])
    for n, (name, src, dst) in enumerate((("feat", feat_h, feat), ("gain", gain_h, gain), ("cot", cot_h, cot))):
        loads[name] = pltpu.make_async_copy(src, dst, wsem.at[7 + n])
    for name in ("feat", ("up", 0), ("sec", 0), "gain", ("out", 0), ("up", 1), ("sec", 1), ("out", 1), "cot"):
        loads[name].start()

    barrier = pltpu.get_barrier_semaphore()
    for stage, n in GROUPS:
        for j in range(1, n):
            pl.semaphore_signal(barrier, inc=1, device_id=group_peer(stage, j), device_id_type=MESH)

    count = counts[0]
    r = iota((C, 128), 0)
    lane = iota((C, 128), 1)

    def picks(source):
        return jnp.concatenate([onehot(lane + 128 * t == source) for t in range(4)], axis=1)

    comp = (r & 31) * 16 + (r >> 5)
    to_comp = picks(comp)
    loads["feat"].wait()
    xb[0] = dot(to_comp, feat[...]).astype(BF16)

    made = set()

    def order_of(k):
        if k not in made:
            made.add(k)
            if k == 3:
                pt[k] = picks(r ^ (c << 8))
            else:
                digits = ((r >> 6) & 3, (r >> 4) & 3, (r >> 2) & 3)
                held = {ORDER[k][n]: digits[n] for n in range(3)}
                pt[k] = picks(held[0] * 128 + ((r >> 8) ^ c) * 64 + held[1] * 16 + held[2] * 4 + (r & 3))
        return pt[k]

    eye_e = onehot(iota((EDGES, EDGES), 0) == iota((EDGES, EDGES), 1))
    row = jnp.concatenate([send[s : s + 1, :] for s in range(4)], axis=1)
    scatter = onehot(iota((ATOMS, EDGES), 0) == row)
    gather = dot_nt(eye_e, scatter).astype(BF16)
    ang2 = jnp.concatenate([ang[:, s, :] for s in range(4)], axis=1)
    basis2 = jnp.concatenate([basis[:, s, :] for s in range(4)], axis=1)
    ang_t = jnp.transpose(ang2)
    for m in range(16):
        abc[m] = jnp.broadcast_to(ang_t[:, m : m + 1], (EDGES, 128))
    basis_t = jnp.transpose(basis2)
    wfp[...] = jnp.zeros_like(wfp)
    for layer in (0, 1):
        wfp[layer, :, 64 * layer : 64 * layer + 64] = w_first[layer]
        wsec[layer, 64 * (1 - layer) : 64 * (1 - layer) + 64, :] = jnp.zeros((64, 2048), BF16)

    def edge_rows(s):
        return pl.ds(s * ATOMS, ATOMS)

    def comp_rows(m):
        return pl.ds(m * ATOMS, ATOMS)

    def lanes(t, base=0):
        return pl.ds(pl.multiple_of(base + t * 128, 128), 128)

    def each_tile(body):
        def step(t, carry):
            body(t)
            return carry

        lax.fori_loop(0, 4, step, 0)

    for layer in (0, 1):
        loads["sec", layer].wait()
        p = dot(basis_t, wfp[layer], HIGH)
        pre[layer] = p
        hid[layer] = (p * jax.nn.sigmoid(p)).astype(BF16)
        for d in range(4):
            rad[layer, :, d * C : (d + 1) * C] = dot(hid[layer], wsec[layer, :, d * C : (d + 1) * C])
        loads["up", layer].wait()
        for d, (a, b) in enumerate(LEVELS):
            lbuf[rows_of(a, b), :] = dot(xb[layer, rows_of(a, b), :], wup[layer, d]).astype(BF16)
        for m in range(16):
            lg[layer, m] = dot(gather, lbuf[comp_rows(m), :]).astype(BF16)

        def message(t, layer=layer):
            src0 = [lg[layer, 0, edge_rows(s), lanes(t)].astype(F32) for s in range(4)]
            for d, (a, b) in enumerate(LEVELS):
                weight = [rad[layer, edge_rows(s), lanes(t, d * C)] for s in range(4)]
                from0 = [weight[s] * src0[s] for s in range(4)]
                for m in range(a, b):
                    total = jnp.zeros((ATOMS, 128), F32)
                    for s in range(4):
                        src = lg[layer, m, edge_rows(s), lanes(t)].astype(F32)
                        total += abc[m, edge_rows(s), :] * from0[s] + weight[s] * src
                    sm[layer, comp_rows(m), lanes(t)] = (total * 0.25).astype(BF16)

        each_tile(message)
        loads["out", layer].wait()
        for d, (a, b) in enumerate(LEVELS):
            mx[layer, rows_of(a, b), :] = dot(sm[layer, rows_of(a, b), :], wout[layer, d])
        if layer == 0:
            kind_t = onehot(iota((128, ATOMS), 0) == spec[...])
            eye_a = onehot(iota((ATOMS, ATOMS), 0) == iota((ATOMS, ATOMS), 1))
            kind = dot_nt(eye_a, kind_t)
            kind_b = kind.astype(BF16)
            gpad[...] = jnp.zeros_like(gpad)
            loads["gain"].wait()
            for k in (0, 1):
                gpad[k, 0:89, :] = gain[:, k, :]
                grow[k] = dot(kind, gpad[k], HIGH)

            def gated(t):
                gate = jax.nn.sigmoid(mx[0, 0:ATOMS, lanes(t)])
                skip_gain = grow[0, :, lanes(t)]
                for m in range(16):
                    value = mx[0, comp_rows(m), lanes(t)] * gate
                    value += skip_gain * xb[0, comp_rows(m), lanes(t)].astype(F32)
                    xb[1, comp_rows(m), lanes(t)] = value.astype(BF16)

            each_tile(gated)
    to_comp_live = picks(jnp.where((r & 31) < count, comp, -1))
    loads["cot"].wait()
    dyb[...] = dot(to_comp_live, cot[...])

    def bufs(u):
        if u == SEC:
            return own_s, outb_s, rx0_s, rx1_s, rx2_s, f2_s, 1024
        if u == GAIN:
            return own_g, outb_g, rx0_g, rx1_g, rx2_g, f2_g, 256
        return own.at[u], outb.at[u % OUT_SLOTS], rx0.at[u], rx1.at[u], rx2.at[u], f2.at[u], 256

    def step0(u):
        _, out_r, r0, _, _, _, _ = bufs(u)
        return pltpu.make_async_remote_copy(
            src_ref=out_r, dst_ref=r0, send_sem=ss0.at[u], recv_sem=rs0.at[u],
            device_id=peer(3, 1), device_id_type=MESH,
        )

    def chunk(ref, rows, which, part, parts):
        size = rows // 4 // parts
        return ref.at[pl.ds(pl.multiple_of(which * (rows // 4) + part * size, size), size)]

    def step1(u):
        o, _, _, r1, _, _, rows = bufs(u)
        axis = ORDER[CLASS[u]][0]
        p = along(axis)
        plan = (
            ((p + 2) % 4, 0, 1), ((p + 1) % 4, 1, 1),
            ((p + 2) % 4, 1, 3), ((p + 3) % 4, 0, 3),
            ((p + 1) % 4, 0, 1), ((p + 3) % 4, 1, 3),
        )
        return [
            pltpu.make_async_remote_copy(
                src_ref=chunk(o, rows, which, part, 2), dst_ref=r1.at[n],
                send_sem=ss1.at[6 * u + n], recv_sem=rs1.at[6 * u + n],
                device_id=peer(axis, way), device_id_type=MESH,
            )
            for n, (which, part, way) in enumerate(plan)
        ]

    def step2(u):
        o, _, _, _, r2, _, rows = bufs(u)
        first, second, _ = ORDER[CLASS[u]]
        p1, p2 = along(first), along(second)
        size = rows // 16
        return [
            pltpu.make_async_remote_copy(
                src_ref=o.at[pl.ds(pl.multiple_of(p1 * (rows // 4) + ((p2 + j) % 4) * size, size), size)],
                dst_ref=r2.at[j - 1],
                send_sem=ss2.at[3 * u + j - 1], recv_sem=rs2.at[3 * u + j - 1],
                device_id=peer(second, j), device_id_type=MESH,
            )
            for j in (1, 2, 3)
        ]

    def step3(n):
        if n < NPAIRS:
            k, src, dst = CLASS[PAIRS[n][0]], s3.at[n], rx3.at[n]
        elif n == NPAIRS:
            k, src, dst = 2, s3_s, rx3_s
        else:
            k, src, dst = 2, s3_g, rx3_g
        axis = ORDER[k][2]
        p = along(axis)
        return [
            pltpu.make_async_remote_copy(
                src_ref=src.at[(p + j) % 4], dst_ref=dst.at[j - 1],
                send_sem=ss3.at[3 * n + j - 1], recv_sem=rs3.at[3 * n + j - 1],
                device_id=peer(axis, j), device_id_type=MESH,
            )
            for j in (1, 2, 3)
        ]

    def start(copies):
        for one in copies:
            one.start()

    done2 = set()

    def service(tick):
        u = tick
        if u < NUNITS:
            start([step0(u)])
        u = tick - D0
        if 0 <= u < NUNITS:
            o, _, r0, _, _, _, rows = bufs(u)
            step0(u).wait_recv()
            o[...] = o[...] + r0[...]
            start(step1(u)[:4])
        u = tick - D1
        if 0 <= u < NUNITS:
            o, _, _, r1, _, _, rows = bufs(u)
            copies = step1(u)
            p = along(ORDER[CLASS[u]][0])
            for first, second, which, part in ((0, 4, (p + 1) % 4, 0), (2, 5, (p + 3) % 4, 1)):
                copies[first].wait_recv()
                view = chunk(o, rows, which, part, 2)
                view[...] = view[...] + r1[first]
                start([copies[second]])
        u = tick - D2
        if 0 <= u < NUNITS:
            o, _, _, r1, _, _, rows = bufs(u)
            copies = step1(u)
            p = along(ORDER[CLASS[u]][0])
            for direct, summed, part in ((3, 4, 0), (1, 5, 1)):
                copies[direct].wait_recv()
                copies[summed].wait_recv()
                view = chunk(o, rows, p, part, 2)
                view[...] = view[...] + r1[direct] + r1[summed]
            start(step2(u))
        u = tick - D3
        if 0 <= u < NUNITS:
            o, _, _, _, r2, ff, rows = bufs(u)
            first, second, _ = ORDER[CLASS[u]]
            for copy in step2(u):
                copy.wait_recv()
            size = rows // 16
            at = pl.multiple_of(along(first) * (rows // 4) + along(second) * size, size)
            value = o[pl.ds(at, size)] + r2[0] + r2[1] + r2[2]
            if u == SEC:
                for n in range(4):
                    s3_s[n] = value[16 * n : 16 * n + 16]
                start(step3(NPAIRS))
            elif u == GAIN:
                for n in range(4):
                    s3_g[n] = jnp.concatenate(
                        [value[4 * n : 4 * n + 4, 0:128], value[4 * n : 4 * n + 4, 128:256]], axis=0
                    )
                start(step3(NPAIRS + 1))
            else:
                ff[...] = value
                done2.add(u)
                for n, (ua, ub) in enumerate(PAIRS):
                    if u in (ua, ub) and ua in done2 and ub in done2:
                        va, vb = f2[ua], f2[ub]
                        for q in range(4):
                            s3[n, q] = jnp.concatenate([va[4 * q : 4 * q + 4], vb[4 * q : 4 * q + 4]], axis=0)
                        start(step3(n))

    def put(u, a, g):
        rows = a.shape[0]
        xt[:, 0:rows] = dot_nt(order_of(CLASS[u]), a).astype(BF16)
        if u >= OUT_SLOTS:
            step0(u - OUT_SLOTS).wait_send()
        o, out_r = bufs(u)[:2]
        value = dot(xt[:, 0:rows], g)
        o[...] = value[0:256]
        out_r[...] = value[256:512]

    tick = 0
    for layer in (1, 0):
        def gates(t, layer=layer):
            scalar = mx[layer, 0:ATOMS, lanes(t)]
            gate = jax.nn.sigmoid(scalar)
            dy0 = dyb[0:ATOMS, lanes(t)]
            dgate = jnp.zeros((ATOMS, 128), F32)
            dskip = dy0 * xb[layer, 0:ATOMS, lanes(t)].astype(F32)
            for m in range(1, 16):
                dy = dyb[comp_rows(m), lanes(t)]
                dmx[comp_rows(m), lanes(t)] = (dy * gate).astype(BF16)
                dgate += dy * mx[layer, comp_rows(m), lanes(t)]
                dskip += dy * xb[layer, comp_rows(m), lanes(t)].astype(F32)
            slope = gate * (1.0 - gate)
            dmx[0:ATOMS, lanes(t)] = (dy0 * (gate + scalar * slope) + dgate * slope).astype(BF16)
            dsk[layer, :, lanes(t)] = dskip

        each_tile(gates)
        if layer == 1:
            pl.semaphore_wait(barrier, 22)
        for d, (a, b) in enumerate(LEVELS):
            put(tick, sm[layer, rows_of(a, b), :], dmx[rows_of(a, b), :])
            service(tick)
            tick += 1
        for d, (a, b) in enumerate(LEVELS):
            dsb[rows_of(a, b), :] = dot_nt(dmx[rows_of(a, b), :], wout[layer, d]) * 0.25

        def back(t, layer=layer):
            for s in range(4):
                src0 = lg[layer, 0, edge_rows(s), lanes(t)].astype(F32)
                total0 = jnp.zeros((ATOMS, 128), F32)
                for d, (a, b) in enumerate(LEVELS):
                    weight = rad[layer, edge_rows(s), lanes(t, d * C)]
                    by_harm = jnp.zeros((ATOMS, 128), F32)
                    by_src = jnp.zeros((ATOMS, 128), F32)
                    for m in range(a, b):
                        dt = dsb[comp_rows(m), lanes(t)]
                        by_harm += abc[m, edge_rows(s), :] * dt
                        if m == 0:
                            by_src += dt * src0
                            total0 += dt * weight
                        else:
                            by_src += dt * lg[layer, m, edge_rows(s), lanes(t)].astype(F32)
                            lg[layer, m, edge_rows(s), lanes(t)] = (dt * weight).astype(BF16)
                    dr[layer, edge_rows(s), lanes(t, d * C)] = (by_harm * src0 + by_src).astype(BF16)
                    total0 += weight * by_harm
                lg[layer, 0, edge_rows(s), lanes(t)] = total0.astype(BF16)

        each_tile(back)
        for m in range(16):
            dl[comp_rows(m), :] = dot(scatter, lg[layer, m]).astype(BF16)

        for d, (a, b) in enumerate(LEVELS):
            put(tick, xb[layer, rows_of(a, b), :], dl[rows_of(a, b), :])
            service(tick)
            tick += 1
        for d, (a, b) in enumerate(LEVELS):
            dsb[rows_of(a, b), :] = dot_nt(dl[rows_of(a, b), :], wup[layer, d])

        def skip(t, layer=layer):
            skip_gain = grow[layer, :, lanes(t)]
            for m in range(16):
                dyb[comp_rows(m), lanes(t)] = (
                    dsb[comp_rows(m), lanes(t)] + skip_gain * dyb[comp_rows(m), lanes(t)]
                )

        each_tile(skip)

    first_term = jnp.zeros((8, 128), F32)
    for layer in (0, 1):
        for d in range(4):
            drt[layer, d] = dot_nt(order_of(3), dr[layer, :, d * C : (d + 1) * C]).astype(BF16)
        dhid = dot_nt(dr[layer], wsec[layer])
        p = pre[layer]
        sg = jax.nn.sigmoid(p)
        dpre = dhid * (sg * (1.0 + p * (1.0 - sg)))
        first_term += dot(basis2, dpre, HIGH)
    red[0, 0:8] = first_term
    for d in range(4):
        blk = dot(drt[0, d], hid[0]) + dot(drt[1, d], hid[1])
        own_s[256 * d : 256 * d + 256, :] = blk[0:256]
        outb_s[256 * d : 256 * d + 256, :] = blk[256:512]
    service(tick)
    tick += 1
    for layer in (0, 1):
        hi = dsk[layer].astype(BF16)
        lo = (dsk[layer] - hi.astype(F32)).astype(BF16)
        blk = dot(dot_nt(order_of(2), hi).astype(BF16), kind_b) + dot(dot_nt(order_of(2), lo).astype(BF16), kind_b)
        own_g[:, 128 * layer : 128 * layer + 128] = blk[0:256]
        outb_g[:, 128 * layer : 128 * layer + 128] = blk[256:512]
    service(tick)
    tick += 1

    fgb[...] = dot(picks((r & 15) * 32 + (r >> 4)), dyb[...].astype(BF16)).astype(BF16)
    save = pltpu.make_async_copy(fgb, fg_o, wsem.at[6])
    save.start()

    def all_sum(stage, n):
        p = lax.axis_index("inner") if stage == 0 else lax.axis_index("outer")
        base = 8 * stage

        def copy(j, slot):
            return pltpu.make_async_remote_copy(
                src_ref=red.at[stage], dst_ref=redrx.at[base + slot],
                send_sem=ssr.at[base + j], recv_sem=rsr.at[base + slot],
                device_id=group_peer(stage, j), device_id_type=MESH,
            )

        return [copy(j, p) for j in range(1, n)], [copy(j, (p + j) % n) for j in range(1, n)], base, p

    while tick < NUNITS + D3:
        service(tick)
        tick += 1

    squares = jnp.zeros((8, 128), F32)
    for n in range(NPAIRS + 2):
        if n < NPAIRS:
            src, rec, out, k = s3.at[n], rx3.at[n], fin.at[n], CLASS[PAIRS[n][0]]
        elif n == NPAIRS:
            src, rec, out, k = s3_s, rx3_s, fin_s, 2
        else:
            src, rec, out, k = s3_g, rx3_g, fin_g, 2
        for copy in step3(n):
            copy.wait_recv()
        value = src[along(ORDER[k][2])] + rec[0] + rec[1] + rec[2]
        out[...] = value
        sq = value * value
        if n < NPAIRS:
            for q in range(4):
                squares += sq[:, 128 * q : 128 * q + 128]
        elif n == NPAIRS:
            squares += sq[0:8] + sq[8:16]
        else:
            squares += sq
    red[0, 8:16] = squares
    for stage, n in GROUPS:
        copies, waits, base, p = all_sum(stage, n)
        for one in copies:
            one.start()
        redrx[base + p] = red[stage]
        if stage == 0:
            for u in range(NUNITS):
                if not (u < 16 and u + OUT_SLOTS < 16):
                    step0(u).wait_send()
                for copy in step1(u) + step2(u):
                    copy.wait_send()
            for q in range(NPAIRS + 2):
                for copy in step3(q):
                    copy.wait_send()
        for one in waits:
            one.wait_recv()
        value = redrx[base]
        for j in range(1, n):
            value = value + redrx[base + j]
        red[stage + 1] = value
    sums[...] = red[2]

    for stage, n in GROUPS:
        for copy in all_sum(stage, n)[0]:
            copy.wait_send()
    save.wait()


def finish(fin, fin_s, fin_g, sums, fg, up_o, first_o, sec_o, out_o, gain_o, fg_o):
    fg_o[...] = fg[...]
    first_sum = sums[0:8]
    total = sums[8:16] + first_sum * first_sum
    total = jnp.sum(jnp.sum(total, axis=1, keepdims=True), axis=0, keepdims=True)
    scale = jnp.minimum(1.0, CLIP_NORM / jnp.sqrt(total + 1e-6))
    for n, pair in enumerate(PAIRS):
        value = fin[n] * scale
        for half, u in enumerate(pair):
            which, layer, d = MATS[u]
            ref = up_o if which == "up" else out_o
            ref[layer, d] = value[4 * half : 4 * half + 4]
    scaled = first_sum * scale
    second = fin_s[...] * scale
    gains = fin_g[...] * scale
    for layer in (0, 1):
        first_o[layer] = scaled[:, 64 * layer : 64 * layer + 64]
        sec_o[layer] = second[:, 64 * layer : 64 * layer + 64]
        gain_o[layer] = gains[4 * layer : 4 * layer + 4, 0:89]


def per_device(features, cotangent, counts, senders, angular, basis, species, w_up, w_first, w_second, w_out, gain):
    vm, hbm = pl.BlockSpec(memory_space=pltpu.VMEM), pl.BlockSpec(memory_space=pl.ANY)
    V = pltpu.VMEM
    dma = pltpu.SemaphoreType.DMA
    scratch = [
        V((C, C), BF16), V((C, C), BF16), V((89, 2, C), F32),
        V((2, 4, C, C), BF16), V((2, 4, C, C), BF16), V((2, 128, 2048), BF16), V((2, 8, 128), F32), V((2, 128, C), F32), dma((10,)),
        V((2, C, C), BF16),
        V((2, 16, EDGES, C), BF16),
        V((2, EDGES, 2048), F32),
        V((2, EDGES, 128), F32),
        V((2, EDGES, 128), BF16),
        V((2, C, C), BF16),
        V((2, C, C), F32),
        V((2, ATOMS, C), F32),
        V((16, EDGES, 128), F32),
        V((C, C), BF16),
        V((C, C), F32),
        V((C, C), BF16),
        V((C, C), F32),
        V((2, EDGES, 2048), BF16),
        V((C, C), BF16),
        V((2, 4, C, EDGES), BF16),
        V((C, 256), BF16),
        V((4, C, C), BF16),
        V((2, ATOMS, C), F32),
        V((C, C), BF16),
        V((16, 256, C), F32), V((1024, 128), F32), V((256, 256), F32),
        V((OUT_SLOTS, 256, C), F32), V((1024, 128), F32), V((256, 256), F32),
        V((16, 256, C), F32), V((1024, 128), F32), V((256, 256), F32),
        V((16, 6, 32, C), F32), V((6, 128, 128), F32), V((6, 32, 256), F32),
        V((16, 3, 16, C), F32), V((3, 64, 128), F32), V((3, 16, 256), F32),
        V((16, 16, C), F32), V((64, 128), F32), V((16, 256), F32),
        V((NPAIRS, 4, 8, C), F32), V((4, 16, 128), F32), V((4, 8, 128), F32),
        V((NPAIRS, 3, 8, C), F32), V((3, 16, 128), F32), V((3, 8, 128), F32),
        V((3, 16, 128), F32), V((24, 16, 128), F32),
        dma((NUNITS,)), dma((NUNITS,)), dma((6 * NUNITS,)), dma((6 * NUNITS,)),
        dma((3 * NUNITS,)), dma((3 * NUNITS,)), dma((3 * (NPAIRS + 2),)), dma((3 * (NPAIRS + 2),)),
        dma((24,)), dma((24,)),
    ]
    shape = jax.ShapeDtypeStruct
    sums = pl.pallas_call(
        kernel,
        name="interaction_grads",
        out_shape=(
            shape((NPAIRS, 8, C), F32), shape((16, 128), F32), shape((8, 128), F32), shape((16, 128), F32),
            shape((C, C), BF16),
        ),
        in_specs=[pl.BlockSpec(memory_space=pltpu.SMEM)] + [vm] * 5 + [hbm] * 6,
        out_specs=(vm,) * 4 + (hbm,),
        scratch_shapes=scratch,
        compiler_params=pltpu.CompilerParams(
            collective_id=0, has_side_effects=True, vmem_limit_bytes=63 * 2**20
        ),
        cost_estimate=pl.CostEstimate(flops=8 * 10**9, bytes_accessed=12 * 10**6, transcendentals=10**5),
    )(
        counts, senders, angular, basis, species.reshape(1, ATOMS), w_first,
        features.reshape(C, C), cotangent.reshape(C, C), jnp.transpose(gain, (1, 0, 2)), w_up, w_second, w_out,
    )
    up, first, second, out, gain_grad, feature_grad = pl.pallas_call(
        finish,
        name="clip",
        out_shape=(
            shape((2, 4, 4, C), F32), shape((2, 8, 64), F32), shape((2, 16, 64), F32),
            shape((2, 4, 4, C), F32), shape((2, 4, 89), F32), shape((C, C), BF16),
        ),
        in_specs=[vm] * 5,
        out_specs=(vm,) * 6,
    )(*sums)
    return (
        up, first, jnp.transpose(second, (0, 2, 1)), out, jnp.transpose(gain_grad, (0, 2, 1)),
        feature_grad.reshape(features.shape),
    )


def solution(mesh):
    both = ("inner", "outer")
    return jax.shard_map(
        per_device,
        mesh=mesh,
        in_specs=(
            P(both, None, None), P(both, None, None), P(both), P(None, both), P(None, None, both),
            P(None, None, both), P(both), P(), P(), P(), P(), P(),
        ),
        out_specs=(
            P(None, None, both, None), P(), P(None, None, both), P(None, None, both, None),
            P(None, None, both), P(both, None, None),
        ),
        check_vma=False,
    )
```

```python
import functools

import jax
import jax.numpy as jnp
from jax import lax
from jax.experimental import pallas as pl
from jax.experimental.pallas import tpu as pltpu
from jax.sharding import PartitionSpec as P

MESH = pl.DeviceIdType.MESH
F32, BF16, I32 = jnp.float32, jnp.bfloat16, jnp.int32
HIGH = lax.Precision.HIGHEST
CLIP_NORM = 2048.0

LEVELS = ((0, 1), (1, 4), (4, 9), (9, 16))
ATOMS = 32
EDGES = 128
C = 512

MATS = (
    [("out", 1, d) for d in range(4)]
    + [("up", 1, d) for d in range(4)]
    + [("out", 0, d) for d in range(4)]
    + [("up", 0, d) for d in range(4)]
)
CLASS = [q % 3 for q in range(16)]
CLASS[14] = 1
SEC, GAIN = 16, 17
CLASS = CLASS + [2, 2]
NUNITS = 18
ORDER = ((2, 0, 1), (1, 2, 0), (0, 1, 2))
PAIRS = []
for _k in range(3):
    _own = [q for q in range(16) if CLASS[q] == _k]
    PAIRS += [(_own[n], _own[n + 1]) for n in range(0, len(_own), 2)]
NPAIRS = len(PAIRS)
STEPS = (
    "G1", "P0", "P1", "P2", "P3", "S1", "K4", "A0", "K5", "K6", "K7", "A1", "L1", "P4", "A2", "P5", "A3", "P6", "P7",
    "B0", "X1", "B1", "A4", "G0", "A5", "P8", "B2", "A6", "P9", "B3", "P10", "A7", "P11", "A8", "S0", "C1", "K0",
    "A9", "B5", "K1", "K2", "K3", "B4", "A10", "C0", "P16", "A11", "L0", "B6", "P12", "P13", "C2", "P14", "B7",
    "A16", "P15", "B8", "P17", "A12", "C3", "X0", "A13", "R0", "A14", "C4", "F0", "A15", "C5", "A17", "D1", "B10",
    "B9", "D0", "B11", "C6", "D2", "C7", "B12", "B16", "B13", "C8", "D4", "B14", "B15", "D3", "B17", "C9", "D5",
    "C11", "C10", "D7", "D6", "C13", "C12", "C16", "C15", "E3", "D8", "C17", "C14", "E6", "D9", "E0", "D10", "D12",
    "D11", "D13", "D15", "D16", "D14", "E4", "D17", "E1", "E7", "E8", "E2", "E5", "E9",
)
OUT_SLOTS = 4


def dot(a, b, precision=None):
    return lax.dot_general(
        a, b, (((1,), (0,)), ((), ())), precision=precision, preferred_element_type=F32
    )


def dot_nt(a, b, precision=None):
    return lax.dot_general(
        a, b, (((1,), (1,)), ((), ())), precision=precision, preferred_element_type=F32
    )


GROUPS = ((0, 8), (1, 16))


def dot_tn(a, b):
    return lax.dot_general(a, b, (((0,), (0,)), ((), ())), preferred_element_type=F32)


def position():
    inner, outer = lax.axis_index("inner"), lax.axis_index("outer")
    return inner // 2, inner % 2, outer // 4, outer % 4


def peer(axis, step):
    x, c, z, y = position()
    if axis == 0:
        x = (x + step) % 4
    elif axis == 1:
        z = (z + step) % 4
    elif axis == 2:
        y = (y + step) % 4
    else:
        c = 1 - c
    return (x * 2 + c, z * 4 + y)


def group_peer(stage, step):
    inner, outer = lax.axis_index("inner"), lax.axis_index("outer")
    if stage == 0:
        return ((inner + step) % 8, outer)
    return (inner, (outer + step) % 16)


def along(axis):
    x, c, z, y = position()
    return (x, z, y, c)[axis]


def rows_of(first, last):
    return slice(first * ATOMS, last * ATOMS)


def iota(shape, dim):
    return lax.broadcasted_iota(I32, shape, dim)


def onehot(mask):
    return jnp.where(mask, 1.0, 0.0).astype(BF16)


def kernel(
    counts, send, ang, basis, spec, w_first, feat_h, cot_h, gain_h, wup_h, wsec_h, wout_h,
    fin, fin_s, fin_g, sums, fg_o,
    feat, cot, gain, wup, wout, wsec, wfp, gpad, wsem,
    xb, lg, rad, pre, hid, sm, mx, grow, abc, lbuf, dyb, dmx, dsb, dr, dl, turn, xt, pt, dsk, fgb,
    own, own_s, own_g, outb, outb_s, outb_g,
    rx0, rx0_s, rx0_g, rx1, rx1_s, rx1_g, rx2, rx2_s, rx2_g,
    f2, f2_s, f2_g, s3, s3_s, s3_g, rx3, rx3_s, rx3_g,
    red, redrx,
    ss0, rs0, ss1, rs1, ss2, rs2, ss3, rs3, ssr, rsr,
):
    x, c, z, y = position()

    loads = {}
    for layer in (0, 1):
        loads["up", layer] = pltpu.make_async_copy(wup_h.at[layer], wup.at[layer], wsem.at[3 * layer])
        loads["sec", layer] = pltpu.make_async_copy(
            wsec_h.at[layer], wsec.at[layer, pl.ds(64 * layer, 64)], wsem.at[3 * layer + 1]
        )
        loads["out", layer] = pltpu.make_async_copy(wout_h.at[layer], wout.at[layer], wsem.at[3 * layer + 2])
    for n, (name, src, dst) in enumerate((("feat", feat_h, feat), ("gain", gain_h, gain), ("cot", cot_h, cot))):
        loads[name] = pltpu.make_async_copy(src, dst, wsem.at[7 + n])
    for name in ("feat", ("up", 0), ("sec", 0)):
        loads[name].start()

    barrier = pltpu.get_barrier_semaphore()
    for stage, n in GROUPS:
        for j in range(1, n):
            pl.semaphore_signal(barrier, inc=1, device_id=group_peer(stage, j), device_id_type=MESH)

    count = counts[0]
    r = iota((C, 128), 0)
    lane = iota((C, 128), 1)

    def picks(source):
        return jnp.concatenate([onehot(lane + 128 * t == source) for t in range(4)], axis=1)

    comp = (r & 31) * 16 + (r >> 5)
    to_comp = picks(comp)
    loads["feat"].wait()
    xb[0] = dot(to_comp, feat[...]).astype(BF16)

    made = set()

    def order_of(k):
        if k not in made:
            made.add(k)
            digits = ((r >> 6) & 3, (r >> 4) & 3, (r >> 2) & 3)
            held = {ORDER[k][n]: digits[n] for n in range(3)}
            pt[k] = picks(held[0] * 128 + ((r >> 8) ^ c) * 64 + held[1] * 16 + held[2] * 4 + (r & 3))
        return pt[k]

    eye_e = onehot(iota((EDGES, EDGES), 0) == iota((EDGES, EDGES), 1))
    row = jnp.concatenate([send[s : s + 1, :] for s in range(4)], axis=1)
    scatter = onehot(iota((ATOMS, EDGES), 0) == row)
    gather = dot_nt(eye_e, scatter).astype(BF16)
    ang2 = jnp.concatenate([ang[:, s, :] for s in range(4)], axis=1)
    basis2 = jnp.concatenate([basis[:, s, :] for s in range(4)], axis=1)
    ang_t = jnp.transpose(ang2)
    for m in range(16):
        abc[m] = jnp.broadcast_to(ang_t[:, m : m + 1], (EDGES, 128))
    basis_t = jnp.transpose(basis2)
    wfp[...] = jnp.zeros_like(wfp)
    for layer in (0, 1):
        wfp[layer, :, 64 * layer : 64 * layer + 64] = w_first[layer]
        wsec[layer, 64 * (1 - layer) : 64 * (1 - layer) + 64, :] = jnp.zeros((64, 2048), BF16)

    def edge_rows(s):
        return pl.ds(s * ATOMS, ATOMS)

    def comp_rows(m):
        return pl.ds(m * ATOMS, ATOMS)

    def lanes(t, base=0):
        if isinstance(t, int):
            return pl.ds(base + t * 128, 128)
        return pl.ds(pl.multiple_of(base + t * 128, 128), 128)

    def each_tile(body):
        def step(t, carry):
            body(t)
            return carry

        lax.fori_loop(0, 4, step, 0)

    for layer in (0, 1):
        loads["sec", layer].wait()
        p = dot(basis_t, wfp[layer], HIGH)
        pre[layer] = p
        hid[layer] = (p * jax.nn.sigmoid(p)).astype(BF16)
        for d in range(4):
            rad[layer, :, d * C : (d + 1) * C] = dot(hid[layer], wsec[layer, :, d * C : (d + 1) * C])
        loads["up", layer].wait()
        if layer == 0:
            for name in (("out", 0), "gain", ("up", 1), ("sec", 1)):
                loads[name].start()
        for d, (a, b) in enumerate(LEVELS):
            lbuf[rows_of(a, b), :] = dot(xb[layer, rows_of(a, b), :], wup[layer, d]).astype(BF16)
        for m in range(16):
            lg[layer, m] = dot(gather, lbuf[comp_rows(m), :]).astype(BF16)

        def message(t, layer=layer):
            src0 = [lg[layer, 0, edge_rows(s), lanes(t)].astype(F32) for s in range(4)]
            for d, (a, b) in enumerate(LEVELS):
                weight = [rad[layer, edge_rows(s), lanes(t, d * C)] for s in range(4)]
                from0 = [weight[s] * src0[s] for s in range(4)]
                for m in range(a, b):
                    total = jnp.zeros((ATOMS, 128), F32)
                    for s in range(4):
                        src = lg[layer, m, edge_rows(s), lanes(t)].astype(F32)
                        total += abc[m, edge_rows(s), :] * from0[s] + weight[s] * src
                    sm[layer, comp_rows(m), lanes(t)] = (total * 0.25).astype(BF16)

        each_tile(message)
        loads["out", layer].wait()
        if layer == 0:
            for name in ("cot", ("out", 1)):
                loads[name].start()
        for d, (a, b) in enumerate(LEVELS):
            mx[layer, rows_of(a, b), :] = dot(sm[layer, rows_of(a, b), :], wout[layer, d])
        if layer == 0:
            kind_t = onehot(iota((128, ATOMS), 0) == spec[...])
            eye_a = onehot(iota((ATOMS, ATOMS), 0) == iota((ATOMS, ATOMS), 1))
            kind = dot_nt(eye_a, kind_t)
            kind_b = kind.astype(BF16)
            gpad[...] = jnp.zeros_like(gpad)
            loads["gain"].wait()
            for k in (0, 1):
                gpad[k, 0:89, :] = gain[:, k, :]
                grow[k] = dot(kind, gpad[k], HIGH)

            def gated(t):
                gate = jax.nn.sigmoid(mx[0, 0:ATOMS, lanes(t)])
                skip_gain = grow[0, :, lanes(t)]
                for m in range(16):
                    value = mx[0, comp_rows(m), lanes(t)] * gate
                    value += skip_gain * xb[0, comp_rows(m), lanes(t)].astype(F32)
                    xb[1, comp_rows(m), lanes(t)] = value.astype(BF16)

            each_tile(gated)
    to_comp_live = picks(jnp.where((r & 31) < count, comp, -1))
    loads["cot"].wait()
    dyb[...] = dot(to_comp_live, cot[...])

    def bufs(u):
        if u == SEC:
            return own_s, outb_s, rx0_s, rx1_s, rx2_s, f2_s, 1024
        if u == GAIN:
            return own_g, outb_g, rx0_g, rx1_g, rx2_g, f2_g, 256
        return own.at[u], outb.at[u % OUT_SLOTS], rx0.at[u], rx1.at[u], rx2.at[u], f2.at[u], 256

    def step0(u):
        _, out_r, r0, _, _, _, _ = bufs(u)
        return pltpu.make_async_remote_copy(
            src_ref=out_r, dst_ref=r0, send_sem=ss0.at[u], recv_sem=rs0.at[u],
            device_id=peer(3, 1), device_id_type=MESH,
        )

    def chunk(ref, rows, which, part, parts):
        size = rows // 4 // parts
        return ref.at[pl.ds(pl.multiple_of(which * (rows // 4) + part * size, size), size)]

    def step1(u):
        o, _, _, r1, _, _, rows = bufs(u)
        axis = ORDER[CLASS[u]][0]
        p = along(axis)
        plan = (
            ((p + 2) % 4, 0, 1), ((p + 1) % 4, 1, 1),
            ((p + 2) % 4, 1, 3), ((p + 3) % 4, 0, 3),
            ((p + 1) % 4, 0, 1), ((p + 3) % 4, 1, 3),
        )
        return [
            pltpu.make_async_remote_copy(
                src_ref=chunk(o, rows, which, part, 2), dst_ref=r1.at[n],
                send_sem=ss1.at[6 * u + n], recv_sem=rs1.at[6 * u + n],
                device_id=peer(axis, way), device_id_type=MESH,
            )
            for n, (which, part, way) in enumerate(plan)
        ]

    def step2(u):
        o, _, _, _, r2, _, rows = bufs(u)
        first, second, _ = ORDER[CLASS[u]]
        p1, p2 = along(first), along(second)
        size = rows // 16
        return [
            pltpu.make_async_remote_copy(
                src_ref=o.at[pl.ds(pl.multiple_of(p1 * (rows // 4) + ((p2 + j) % 4) * size, size), size)],
                dst_ref=r2.at[j - 1],
                send_sem=ss2.at[3 * u + j - 1], recv_sem=rs2.at[3 * u + j - 1],
                device_id=peer(second, j), device_id_type=MESH,
            )
            for j in (1, 2, 3)
        ]

    def step3(n):
        if n < NPAIRS:
            k, src, dst = CLASS[PAIRS[n][0]], s3.at[n], rx3.at[n]
        elif n == NPAIRS:
            k, src, dst = 2, s3_s, rx3_s
        else:
            k, src, dst = 2, s3_g, rx3_g
        axis = ORDER[k][2]
        p = along(axis)
        return [
            pltpu.make_async_remote_copy(
                src_ref=src.at[(p + j) % 4], dst_ref=dst.at[j - 1],
                send_sem=ss3.at[3 * n + j - 1], recv_sem=rs3.at[3 * n + j - 1],
                device_id=peer(axis, j), device_id_type=MESH,
            )
            for j in (1, 2, 3)
        ]

    def start(copies):
        for one in copies:
            one.start()

    done2 = set()

    def from_core(u):
        o, _, r0, _, _, _, _ = bufs(u)
        step0(u).wait_recv()
        o[...] = o[...] + r0[...]
        start(step1(u)[:4])

    def pass_on(u):
        o, _, _, r1, _, _, rows = bufs(u)
        copies = step1(u)
        p = along(ORDER[CLASS[u]][0])
        for first, second, which, part in ((0, 4, (p + 1) % 4, 0), (2, 5, (p + 3) % 4, 1)):
            copies[first].wait_recv()
            view = chunk(o, rows, which, part, 2)
            view[...] = view[...] + r1[first]
            start([copies[second]])

    def end_first(u):
        o, _, _, r1, _, _, rows = bufs(u)
        copies = step1(u)
        p = along(ORDER[CLASS[u]][0])
        for direct, summed, part in ((3, 4, 0), (1, 5, 1)):
            copies[direct].wait_recv()
            copies[summed].wait_recv()
            view = chunk(o, rows, p, part, 2)
            view[...] = view[...] + r1[direct] + r1[summed]
        start(step2(u))

    def end_second(u):
        o, _, _, _, r2, ff, rows = bufs(u)
        first, second, _ = ORDER[CLASS[u]]
        for copy in step2(u):
            copy.wait_recv()
        size = rows // 16
        at = pl.multiple_of(along(first) * (rows // 4) + along(second) * size, size)
        value = o[pl.ds(at, size)] + r2[0] + r2[1] + r2[2]
        if u == SEC:
            for n in range(4):
                s3_s[n] = value[16 * n : 16 * n + 16]
            start(step3(NPAIRS))
        elif u == GAIN:
            for n in range(4):
                s3_g[n] = jnp.concatenate(
                    [value[4 * n : 4 * n + 4, 0:128], value[4 * n : 4 * n + 4, 128:256]], axis=0
                )
            start(step3(NPAIRS + 1))
        else:
            ff[...] = value
            done2.add(u)
            for n, (ua, ub) in enumerate(PAIRS):
                if u in (ua, ub) and ua in done2 and ub in done2:
                    va, vb = f2[ua], f2[ub]
                    for q in range(4):
                        s3[n, q] = jnp.concatenate([va[4 * q : 4 * q + 4], vb[4 * q : 4 * q + 4]], axis=0)
                    start(step3(n))

    red[0] = jnp.zeros((16, 128), F32)

    def end_third(n):
        if n < NPAIRS:
            src, rec, out, k = s3.at[n], rx3.at[n], fin.at[n], CLASS[PAIRS[n][0]]
        elif n == NPAIRS:
            src, rec, out, k = s3_s, rx3_s, fin_s, 2
        else:
            src, rec, out, k = s3_g, rx3_g, fin_g, 2
        for copy in step3(n):
            copy.wait_recv()
        value = src[along(ORDER[k][2])] + rec[0] + rec[1] + rec[2]
        out[...] = value
        sq = value * value
        if n < NPAIRS:
            sq = sq[:, 0:128] + sq[:, 128:256] + sq[:, 256:384] + sq[:, 384:512]
        elif n == NPAIRS:
            sq = sq[0:8] + sq[8:16]
        red[0, 8:16] = red[0, 8:16] + sq

    def put(u, a, g):
        rows = a.shape[0]
        xt[:, 0:rows] = dot_nt(order_of(CLASS[u]), a).astype(BF16)
        if u >= OUT_SLOTS:
            step0(u - OUT_SLOTS).wait_send()
        o, out_r = bufs(u)[:2]
        value = dot(xt[:, 0:rows], g)
        o[...] = value[0:256]
        out_r[...] = value[256:512]
        start([step0(u)])

    def gates(layer):
        def tile(t):
            scalar = mx[layer, 0:ATOMS, lanes(t)]
            gate = jax.nn.sigmoid(scalar)
            dy0 = dyb[0:ATOMS, lanes(t)]
            dgate = jnp.zeros((ATOMS, 128), F32)
            dskip = dy0 * xb[layer, 0:ATOMS, lanes(t)].astype(F32)
            for m in range(1, 16):
                dy = dyb[comp_rows(m), lanes(t)]
                dmx[comp_rows(m), lanes(t)] = (dy * gate).astype(BF16)
                dgate += dy * mx[layer, comp_rows(m), lanes(t)]
                dskip += dy * xb[layer, comp_rows(m), lanes(t)].astype(F32)
            slope = gate * (1.0 - gate)
            dmx[0:ATOMS, lanes(t)] = (dy0 * (gate + scalar * slope) + dgate * slope).astype(BF16)
            dsk[layer, :, lanes(t)] = dskip

        each_tile(tile)
        if layer == 1:
            pl.semaphore_wait(barrier, 22)

    def product(u):
        if u == SEC:
            second_product()
        elif u == GAIN:
            gain_product()
        else:
            which, layer, d = MATS[u]
            rows = rows_of(*LEVELS[d])
            if which == "out":
                put(u, sm[layer, rows, :], dmx[rows, :])
            else:
                put(u, xb[layer, rows, :], dl[rows, :])

    def summed_grad(layer):
        for d, (a, b) in enumerate(LEVELS):
            dsb[rows_of(a, b), :] = dot_nt(dmx[rows_of(a, b), :], wout[layer, d]) * 0.25

    def message_grad(n):
        layer, t = n // 4, n % 4
        for s in range(4):
            src0 = lg[layer, 0, edge_rows(s), lanes(t)].astype(F32)
            total0 = jnp.zeros((ATOMS, 128), F32)
            for d, (a, b) in enumerate(LEVELS):
                weight = rad[layer, edge_rows(s), lanes(t, d * C)]
                by_harm = jnp.zeros((ATOMS, 128), F32)
                by_src = jnp.zeros((ATOMS, 128), F32)
                for m in range(a, b):
                    dt = dsb[comp_rows(m), lanes(t)]
                    by_harm += abc[m, edge_rows(s), :] * dt
                    if m == 0:
                        by_src += dt * src0
                        total0 += dt * weight
                    else:
                        by_src += dt * lg[layer, m, edge_rows(s), lanes(t)].astype(F32)
                        lg[layer, m, edge_rows(s), lanes(t)] = (dt * weight).astype(BF16)
                dr[layer, edge_rows(s), lanes(t, d * C)] = (by_harm * src0 + by_src).astype(BF16)
                total0 += weight * by_harm
            lg[layer, 0, edge_rows(s), lanes(t)] = total0.astype(BF16)

    def lifted_grad(layer):
        for m in range(16):
            dl[comp_rows(m), :] = dot(scatter, lg[layer, m]).astype(BF16)

    def input_grad(layer):
        for d, (a, b) in enumerate(LEVELS):
            dsb[rows_of(a, b), :] = dot_nt(dl[rows_of(a, b), :], wup[layer, d])

        def tile(t):
            skip_gain = grow[layer, :, lanes(t)]
            for m in range(16):
                dyb[comp_rows(m), lanes(t)] = (
                    dsb[comp_rows(m), lanes(t)] + skip_gain * dyb[comp_rows(m), lanes(t)]
                )

        each_tile(tile)

    def radial_grad(_):
        term = jnp.zeros((8, 128), F32)
        for layer in (0, 1):
            dhid = dot_nt(dr[layer], wsec[layer])
            p = pre[layer]
            sg = jax.nn.sigmoid(p)
            term += dot(basis2, dhid * (sg * (1.0 + p * (1.0 - sg))), HIGH)
        red[0, 0:8] = term

    def second_product():
        for d in range(4):
            wide = slice(d * C, (d + 1) * C)
            blk = dot_tn(hid[0], dr[0, :, wide]) + dot_tn(hid[1], dr[1, :, wide])
            turn[...] = jnp.transpose(blk)
            own_s[256 * d : 256 * d + 256, :] = turn[pl.ds(pl.multiple_of(c * 256, 256), 256), :]
            outb_s[256 * d : 256 * d + 256, :] = turn[pl.ds(pl.multiple_of((1 - c) * 256, 256), 256), :]
        start([step0(SEC)])

    def gain_product():
        for layer in (0, 1):
            hi = dsk[layer].astype(BF16)
            lo = (dsk[layer] - hi.astype(F32)).astype(BF16)
            rows = dot_nt(order_of(2), jnp.concatenate([hi, lo], axis=0)).astype(BF16)
            blk = dot(rows, jnp.concatenate([kind_b, kind_b], axis=0))
            own_g[:, 128 * layer : 128 * layer + 128] = blk[0:256]
            outb_g[:, 128 * layer : 128 * layer + 128] = blk[256:512]
        start([step0(GAIN)])

    saves = []

    def feature_grad(_):
        fgb[...] = dot(picks((r & 15) * 32 + (r >> 4)), dyb[...].astype(BF16)).astype(BF16)
        saves.append(pltpu.make_async_copy(fgb, fg_o, wsem.at[6]))
        saves[0].start()

    actions = {
        "G": gates, "P": product, "S": summed_grad, "K": message_grad, "L": lifted_grad, "X": input_grad,
        "R": radial_grad, "F": feature_grad,
        "A": from_core, "B": pass_on, "C": end_first, "D": end_second, "E": end_third,
    }
    for step in STEPS:
        actions[step[0]](int(step[1:]))

    def all_sum(stage, n):
        p = lax.axis_index("inner") if stage == 0 else lax.axis_index("outer")
        base = 8 * stage

        def copy(j, slot):
            return pltpu.make_async_remote_copy(
                src_ref=red.at[stage], dst_ref=redrx.at[base + slot],
                send_sem=ssr.at[base + j], recv_sem=rsr.at[base + slot],
                device_id=group_peer(stage, j), device_id_type=MESH,
            )

        return [copy(j, p) for j in range(1, n)], [copy(j, (p + j) % n) for j in range(1, n)], base, p

    for stage, n in GROUPS:
        copies, waits, base, p = all_sum(stage, n)
        for one in copies:
            one.start()
        redrx[base + p] = red[stage]
        if stage == 0:
            for u in range(NUNITS):
                if not (u < 16 and u + OUT_SLOTS < 16):
                    step0(u).wait_send()
                for copy in step1(u) + step2(u):
                    copy.wait_send()
            for q in range(NPAIRS + 2):
                for copy in step3(q):
                    copy.wait_send()
        for one in waits:
            one.wait_recv()
        value = redrx[base]
        for j in range(1, n):
            value = value + redrx[base + j]
        red[stage + 1] = value
    sums[...] = red[2]

    for stage, n in GROUPS:
        for copy in all_sum(stage, n)[0]:
            copy.wait_send()
    saves[0].wait()


def finish(fin, fin_s, fin_g, sums, fg, up_o, first_o, sec_o, out_o, gain_o, fg_o):
    fg_o[...] = fg[...]
    first_sum = sums[0:8]
    total = sums[8:16] + first_sum * first_sum
    total = jnp.sum(jnp.sum(total, axis=1, keepdims=True), axis=0, keepdims=True)
    scale = jnp.minimum(1.0, CLIP_NORM / jnp.sqrt(total + 1e-6))
    for n, pair in enumerate(PAIRS):
        value = fin[n] * scale
        for half, u in enumerate(pair):
            which, layer, d = MATS[u]
            ref = up_o if which == "up" else out_o
            ref[layer, d] = value[4 * half : 4 * half + 4]
    scaled = first_sum * scale
    second = fin_s[...] * scale
    gains = fin_g[...] * scale
    for layer in (0, 1):
        first_o[layer] = scaled[:, 64 * layer : 64 * layer + 64]
        sec_o[layer] = second[:, 64 * layer : 64 * layer + 64]
        gain_o[layer] = gains[4 * layer : 4 * layer + 4, 0:89]


def per_device(features, cotangent, counts, senders, angular, basis, species, w_up, w_first, w_second, w_out, gain):
    vm, hbm = pl.BlockSpec(memory_space=pltpu.VMEM), pl.BlockSpec(memory_space=pl.ANY)
    V = pltpu.VMEM
    dma = pltpu.SemaphoreType.DMA
    scratch = [
        V((C, C), BF16), V((C, C), BF16), V((89, 2, C), F32),
        V((2, 4, C, C), BF16), V((2, 4, C, C), BF16), V((2, 128, 2048), BF16), V((2, 8, 128), F32), V((2, 128, C), F32), dma((10,)),
        V((2, C, C), BF16),
        V((2, 16, EDGES, C), BF16),
        V((2, EDGES, 2048), F32),
        V((2, EDGES, 128), F32),
        V((2, EDGES, 128), BF16),
        V((2, C, C), BF16),
        V((2, C, C), F32),
        V((2, ATOMS, C), F32),
        V((16, EDGES, 128), F32),
        V((C, C), BF16),
        V((C, C), F32),
        V((C, C), BF16),
        V((C, C), F32),
        V((2, EDGES, 2048), BF16),
        V((C, C), BF16),
        V((C, 128), F32),
        V((C, 256), BF16),
        V((3, C, C), BF16),
        V((2, ATOMS, C), F32),
        V((C, C), BF16),
        V((16, 256, C), F32), V((1024, 128), F32), V((256, 256), F32),
        V((OUT_SLOTS, 256, C), F32), V((1024, 128), F32), V((256, 256), F32),
        V((16, 256, C), F32), V((1024, 128), F32), V((256, 256), F32),
        V((16, 6, 32, C), F32), V((6, 128, 128), F32), V((6, 32, 256), F32),
        V((16, 3, 16, C), F32), V((3, 64, 128), F32), V((3, 16, 256), F32),
        V((16, 16, C), F32), V((64, 128), F32), V((16, 256), F32),
        V((NPAIRS, 4, 8, C), F32), V((4, 16, 128), F32), V((4, 8, 128), F32),
        V((NPAIRS, 3, 8, C), F32), V((3, 16, 128), F32), V((3, 8, 128), F32),
        V((3, 16, 128), F32), V((24, 16, 128), F32),
        dma((NUNITS,)), dma((NUNITS,)), dma((6 * NUNITS,)), dma((6 * NUNITS,)),
        dma((3 * NUNITS,)), dma((3 * NUNITS,)), dma((3 * (NPAIRS + 2),)), dma((3 * (NPAIRS + 2),)),
        dma((24,)), dma((24,)),
    ]
    shape = jax.ShapeDtypeStruct
    sums = pl.pallas_call(
        kernel,
        name="interaction_grads",
        out_shape=(
            shape((NPAIRS, 8, C), F32), shape((16, 128), F32), shape((8, 128), F32), shape((16, 128), F32),
            shape((C, C), BF16),
        ),
        in_specs=[pl.BlockSpec(memory_space=pltpu.SMEM)] + [vm] * 5 + [hbm] * 6,
        out_specs=(vm,) * 4 + (hbm,),
        scratch_shapes=scratch,
        compiler_params=pltpu.CompilerParams(
            collective_id=0, has_side_effects=True, vmem_limit_bytes=63 * 2**20
        ),
        cost_estimate=pl.CostEstimate(flops=8 * 10**9, bytes_accessed=12 * 10**6, transcendentals=10**5),
    )(
        counts, senders, angular, basis, species.reshape(1, ATOMS), w_first,
        features.reshape(C, C), cotangent.reshape(C, C), jnp.transpose(gain, (1, 0, 2)), w_up, w_second, w_out,
    )
    up, first, second, out, gain_grad, feature_grad = pl.pallas_call(
        finish,
        name="clip",
        out_shape=(
            shape((2, 4, 4, C), F32), shape((2, 8, 64), F32), shape((2, 16, 64), F32),
            shape((2, 4, 4, C), F32), shape((2, 4, 89), F32), shape((C, C), BF16),
        ),
        in_specs=[vm] * 5,
        out_specs=(vm,) * 6,
    )(*sums)
    return (
        up, first, jnp.transpose(second, (0, 2, 1)), out, jnp.transpose(gain_grad, (0, 2, 1)),
        feature_grad.reshape(features.shape),
    )


def solution(mesh):
    both = ("inner", "outer")
    return jax.shard_map(
        per_device,
        mesh=mesh,
        in_specs=(
            P(both, None, None), P(both, None, None), P(both), P(None, both), P(None, None, both),
            P(None, None, both), P(both), P(), P(), P(), P(), P(),
        ),
        out_specs=(
            P(None, None, both, None), P(), P(None, None, both), P(None, None, both, None),
            P(None, None, both), P(both, None, None),
        ),
        check_vma=False,
    )
```

```python
import functools

import jax
import jax.numpy as jnp
from jax import lax
from jax.experimental import pallas as pl
from jax.experimental.pallas import tpu as pltpu
from jax.sharding import PartitionSpec as P

MESH = pl.DeviceIdType.MESH
F32, BF16, I32 = jnp.float32, jnp.bfloat16, jnp.int32
HIGH = lax.Precision.HIGHEST
CLIP_NORM = 2048.0

LEVELS = ((0, 1), (1, 4), (4, 9), (9, 16))
ATOMS = 32
EDGES = 128
C = 512

MATS = (
    [("out", 1, d) for d in range(4)]
    + [("up", 1, d) for d in range(4)]
    + [("out", 0, d) for d in range(4)]
    + [("up", 0, d) for d in range(4)]
)
CLASS = [q % 3 for q in range(16)]
CLASS[14] = 1
SEC, GAIN = 16, 17
CLASS = CLASS + [2, 2]
NUNITS = 18
ORDER = ((2, 0, 1), (1, 2, 0), (0, 1, 2))
PAIRS = []
for _k in range(3):
    _own = [q for q in range(16) if CLASS[q] == _k]
    PAIRS += [(_own[n], _own[n + 1]) for n in range(0, len(_own), 2)]
NPAIRS = len(PAIRS)
STEPS = (
    "G1", "P0", "P1", "P2", "P3", "S1", "K4", "A0", "K5", "K6", "K7", "A1", "L1", "P4", "A2", "P5", "A3", "P6", "P7",
    "B0", "X1", "B1", "A4", "G0", "A5", "P8", "B2", "A6", "P9", "B3", "P10", "A7", "P11", "A8", "S0", "C1", "K0",
    "A9", "B5", "K1", "K2", "K3", "B4", "A10", "C0", "P16", "A11", "L0", "B6", "P12", "P13", "C2", "P14", "B7",
    "A16", "P15", "B8", "P17", "A12", "C3", "X0", "A13", "R0", "A14", "C4", "F0", "A15", "C5", "A17", "D1", "B10",
    "B9", "D0", "B11", "C6", "D2", "C7", "B12", "B16", "B13", "C8", "D4", "B14", "B15", "D3", "B17", "C9", "D5",
    "C11", "C10", "D7", "D6", "C13", "C12", "C16", "C15", "E3", "D8", "C17", "C14", "E6", "D9", "E0", "D10", "D12",
    "D11", "D13", "D15", "D16", "D14", "E4", "D17", "E1", "E7", "E8", "E2", "E5", "E9",
)
OUT_SLOTS = 4


def dot(a, b, precision=None):
    return lax.dot_general(
        a, b, (((1,), (0,)), ((), ())), precision=precision, preferred_element_type=F32
    )


def dot_nt(a, b, precision=None):
    return lax.dot_general(
        a, b, (((1,), (1,)), ((), ())), precision=precision, preferred_element_type=F32
    )


GROUPS = ((0, 8), (1, 16))


def dot_tn(a, b):
    return lax.dot_general(a, b, (((0,), (0,)), ((), ())), preferred_element_type=F32)


def position():
    inner, outer = lax.axis_index("inner"), lax.axis_index("outer")
    return inner // 2, inner % 2, outer // 4, outer % 4


def peer(axis, step):
    x, c, z, y = position()
    if axis == 0:
        x = (x + step) % 4
    elif axis == 1:
        z = (z + step) % 4
    elif axis == 2:
        y = (y + step) % 4
    else:
        c = 1 - c
    return (x * 2 + c, z * 4 + y)


def group_peer(stage, step):
    inner, outer = lax.axis_index("inner"), lax.axis_index("outer")
    if stage == 0:
        return ((inner + step) % 8, outer)
    return (inner, (outer + step) % 16)


def along(axis):
    x, c, z, y = position()
    return (x, z, y, c)[axis]


def rows_of(first, last):
    return slice(first * ATOMS, last * ATOMS)


def iota(shape, dim):
    return lax.broadcasted_iota(I32, shape, dim)


def onehot(mask):
    return jnp.where(mask, 1.0, 0.0).astype(BF16)


def kernel(
    counts, send, ang, basis, spec, w_first, feat_h, cot_h, gain_h, wup_h, wsec_h, wout_h,
    fin_h, fin_sh, fin_gh, sums, fg_o,
    feat, cot, gain, wup, wout, wsec, wfp, gpad, wsem,
    xb, lg, rad, pre, hid, sm, mx, grow, abc, lbuf, dyb, dmx, dsb, dr, dl, turn, xt, pt, dsk, fgb,
    own, own_s, own_g, outb, outb_s, outb_g,
    rx0, rx0_s, rx0_g, rx1, rx1_s, rx1_g, rx2, rx2_s, rx2_g,
    f2, f2_s, f2_g, s3, s3_s, s3_g, rx3, rx3_s, rx3_g,
    fin, fin_s, fin_g, red, redrx,
    ss0, rs0, ss1, rs1, ss2, rs2, ss3, rs3, ssr, rsr,
):
    x, c, z, y = position()

    loads = {}
    for layer in (0, 1):
        loads["up", layer] = pltpu.make_async_copy(wup_h.at[layer], wup.at[layer], wsem.at[3 * layer])
        loads["sec", layer] = pltpu.make_async_copy(
            wsec_h.at[layer], wsec.at[layer, pl.ds(64 * layer, 64)], wsem.at[3 * layer + 1]
        )
        loads["out", layer] = pltpu.make_async_copy(wout_h.at[layer], wout.at[layer], wsem.at[3 * layer + 2])
    for n, (name, src, dst) in enumerate((("feat", feat_h, feat), ("gain", gain_h, gain), ("cot", cot_h, cot))):
        loads[name] = pltpu.make_async_copy(src, dst, wsem.at[7 + n])
    for name in ("feat", ("up", 0), ("sec", 0)):
        loads[name].start()

    barrier = pltpu.get_barrier_semaphore()
    for stage, n in GROUPS:
        for j in range(1, n):
            pl.semaphore_signal(barrier, inc=1, device_id=group_peer(stage, j), device_id_type=MESH)

    count = counts[0]
    r = iota((C, 128), 0)
    lane = iota((C, 128), 1)

    def picks(source):
        return jnp.concatenate([onehot(lane + 128 * t == source) for t in range(4)], axis=1)

    comp = (r & 31) * 16 + (r >> 5)
    to_comp = picks(comp)
    loads["feat"].wait()
    xb[0] = dot(to_comp, feat[...]).astype(BF16)

    made = set()

    def order_of(k):
        if k not in made:
            made.add(k)
            digits = ((r >> 6) & 3, (r >> 4) & 3, (r >> 2) & 3)
            held = {ORDER[k][n]: digits[n] for n in range(3)}
            pt[k] = picks(held[0] * 128 + ((r >> 8) ^ c) * 64 + held[1] * 16 + held[2] * 4 + (r & 3))
        return pt[k]

    eye_e = onehot(iota((EDGES, EDGES), 0) == iota((EDGES, EDGES), 1))
    row = jnp.concatenate([send[s : s + 1, :] for s in range(4)], axis=1)
    scatter = onehot(iota((ATOMS, EDGES), 0) == row)
    gather = dot_nt(eye_e, scatter).astype(BF16)
    ang2 = jnp.concatenate([ang[:, s, :] for s in range(4)], axis=1)
    basis2 = jnp.concatenate([basis[:, s, :] for s in range(4)], axis=1)
    ang_t = jnp.transpose(ang2)
    for m in range(16):
        abc[m] = jnp.broadcast_to(ang_t[:, m : m + 1], (EDGES, 128))
    basis_t = jnp.transpose(basis2)
    wfp[...] = jnp.zeros_like(wfp)
    for layer in (0, 1):
        wfp[layer, :, 64 * layer : 64 * layer + 64] = w_first[layer]
        wsec[layer, 64 * (1 - layer) : 64 * (1 - layer) + 64, :] = jnp.zeros((64, 2048), BF16)

    def edge_rows(s):
        return pl.ds(s * ATOMS, ATOMS)

    def comp_rows(m):
        return pl.ds(m * ATOMS, ATOMS)

    def lanes(t, base=0):
        if isinstance(t, int):
            return pl.ds(base + t * 128, 128)
        return pl.ds(pl.multiple_of(base + t * 128, 128), 128)

    def each_tile(body):
        def step(t, carry):
            body(t)
            return carry

        lax.fori_loop(0, 4, step, 0)

    for layer in (0, 1):
        loads["sec", layer].wait()
        p = dot(basis_t, wfp[layer], HIGH)
        pre[layer] = p
        hid[layer] = (p * jax.nn.sigmoid(p)).astype(BF16)
        for d in range(4):
            rad[layer, :, d * C : (d + 1) * C] = dot(hid[layer], wsec[layer, :, d * C : (d + 1) * C])
        loads["up", layer].wait()
        if layer == 0:
            for name in (("out", 0), "gain", ("up", 1), ("sec", 1)):
                loads[name].start()
        for d, (a, b) in enumerate(LEVELS):
            lbuf[rows_of(a, b), :] = dot(xb[layer, rows_of(a, b), :], wup[layer, d]).astype(BF16)
        for m in range(16):
            lg[layer, m] = dot(gather, lbuf[comp_rows(m), :]).astype(BF16)

        def message(t, layer=layer):
            src0 = [lg[layer, 0, edge_rows(s), lanes(t)].astype(F32) for s in range(4)]
            for d, (a, b) in enumerate(LEVELS):
                weight = [rad[layer, edge_rows(s), lanes(t, d * C)] for s in range(4)]
                from0 = [weight[s] * src0[s] for s in range(4)]
                for m in range(a, b):
                    total = jnp.zeros((ATOMS, 128), F32)
                    for s in range(4):
                        src = lg[layer, m, edge_rows(s), lanes(t)].astype(F32)
                        total += abc[m, edge_rows(s), :] * from0[s] + weight[s] * src
                    sm[layer, comp_rows(m), lanes(t)] = (total * 0.25).astype(BF16)

        each_tile(message)
        loads["out", layer].wait()
        if layer == 0:
            for name in ("cot", ("out", 1)):
                loads[name].start()
        for d, (a, b) in enumerate(LEVELS):
            mx[layer, rows_of(a, b), :] = dot(sm[layer, rows_of(a, b), :], wout[layer, d])
        if layer == 0:
            kind_t = onehot(iota((128, ATOMS), 0) == spec[...])
            eye_a = onehot(iota((ATOMS, ATOMS), 0) == iota((ATOMS, ATOMS), 1))
            kind = dot_nt(eye_a, kind_t)
            kind_b = kind.astype(BF16)
            gpad[...] = jnp.zeros_like(gpad)
            loads["gain"].wait()
            for k in (0, 1):
                gpad[k, 0:89, :] = gain[:, k, :]
                grow[k] = dot(kind, gpad[k], HIGH)

            def gated(t):
                gate = jax.nn.sigmoid(mx[0, 0:ATOMS, lanes(t)])
                skip_gain = grow[0, :, lanes(t)]
                for m in range(16):
                    value = mx[0, comp_rows(m), lanes(t)] * gate
                    value += skip_gain * xb[0, comp_rows(m), lanes(t)].astype(F32)
                    xb[1, comp_rows(m), lanes(t)] = value.astype(BF16)

            each_tile(gated)
    to_comp_live = picks(jnp.where((r & 31) < count, comp, -1))
    loads["cot"].wait()
    dyb[...] = dot(to_comp_live, cot[...])

    def bufs(u):
        if u == SEC:
            return own_s, outb_s, rx0_s, rx1_s, rx2_s, f2_s, 1024
        if u == GAIN:
            return own_g, outb_g, rx0_g, rx1_g, rx2_g, f2_g, 256
        return own.at[u], outb.at[u % OUT_SLOTS], rx0.at[u], rx1.at[u], rx2.at[u], f2.at[u], 256

    def step0(u):
        _, out_r, r0, _, _, _, _ = bufs(u)
        return pltpu.make_async_remote_copy(
            src_ref=out_r, dst_ref=r0, send_sem=ss0.at[u], recv_sem=rs0.at[u],
            device_id=peer(3, 1), device_id_type=MESH,
        )

    def chunk(ref, rows, which, part, parts):
        size = rows // 4 // parts
        return ref.at[pl.ds(pl.multiple_of(which * (rows // 4) + part * size, size), size)]

    def step1(u):
        o, _, _, r1, _, _, rows = bufs(u)
        axis = ORDER[CLASS[u]][0]
        p = along(axis)
        plan = (
            ((p + 2) % 4, 0, 1), ((p + 1) % 4, 1, 1),
            ((p + 2) % 4, 1, 3), ((p + 3) % 4, 0, 3),
            ((p + 1) % 4, 0, 1), ((p + 3) % 4, 1, 3),
        )
        return [
            pltpu.make_async_remote_copy(
                src_ref=chunk(o, rows, which, part, 2), dst_ref=r1.at[n],
                send_sem=ss1.at[6 * u + n], recv_sem=rs1.at[6 * u + n],
                device_id=peer(axis, way), device_id_type=MESH,
            )
            for n, (which, part, way) in enumerate(plan)
        ]

    def step2(u):
        o, _, _, _, r2, _, rows = bufs(u)
        first, second, _ = ORDER[CLASS[u]]
        p1, p2 = along(first), along(second)
        size = rows // 16
        return [
            pltpu.make_async_remote_copy(
                src_ref=o.at[pl.ds(pl.multiple_of(p1 * (rows // 4) + ((p2 + j) % 4) * size, size), size)],
                dst_ref=r2.at[j - 1],
                send_sem=ss2.at[3 * u + j - 1], recv_sem=rs2.at[3 * u + j - 1],
                device_id=peer(second, j), device_id_type=MESH,
            )
            for j in (1, 2, 3)
        ]

    def step3(n):
        if n < NPAIRS:
            k, src, dst = CLASS[PAIRS[n][0]], s3.at[n], rx3.at[n]
        elif n == NPAIRS:
            k, src, dst = 2, s3_s, rx3_s
        else:
            k, src, dst = 2, s3_g, rx3_g
        axis = ORDER[k][2]
        p = along(axis)
        return [
            pltpu.make_async_remote_copy(
                src_ref=src.at[(p + j) % 4], dst_ref=dst.at[j - 1],
                send_sem=ss3.at[3 * n + j - 1], recv_sem=rs3.at[3 * n + j - 1],
                device_id=peer(axis, j), device_id_type=MESH,
            )
            for j in (1, 2, 3)
        ]

    def start(copies):
        for one in copies:
            one.start()

    done2 = set()

    def from_core(u):
        o, _, r0, _, _, _, _ = bufs(u)
        step0(u).wait_recv()
        o[...] = o[...] + r0[...]
        start(step1(u)[:4])

    def pass_on(u):
        o, _, _, r1, _, _, rows = bufs(u)
        copies = step1(u)
        p = along(ORDER[CLASS[u]][0])
        for first, second, which, part in ((0, 4, (p + 1) % 4, 0), (2, 5, (p + 3) % 4, 1)):
            copies[first].wait_recv()
            view = chunk(o, rows, which, part, 2)
            view[...] = view[...] + r1[first]
            start([copies[second]])

    def end_first(u):
        o, _, _, r1, _, _, rows = bufs(u)
        copies = step1(u)
        p = along(ORDER[CLASS[u]][0])
        for direct, summed, part in ((3, 4, 0), (1, 5, 1)):
            copies[direct].wait_recv()
            copies[summed].wait_recv()
            view = chunk(o, rows, p, part, 2)
            view[...] = view[...] + r1[direct] + r1[summed]
        start(step2(u))

    def end_second(u):
        o, _, _, _, r2, ff, rows = bufs(u)
        first, second, _ = ORDER[CLASS[u]]
        for copy in step2(u):
            copy.wait_recv()
        size = rows // 16
        at = pl.multiple_of(along(first) * (rows // 4) + along(second) * size, size)
        value = o[pl.ds(at, size)] + r2[0] + r2[1] + r2[2]
        if u == SEC:
            for n in range(4):
                s3_s[n] = value[16 * n : 16 * n + 16]
            start(step3(NPAIRS))
        elif u == GAIN:
            for n in range(4):
                s3_g[n] = jnp.concatenate(
                    [value[4 * n : 4 * n + 4, 0:128], value[4 * n : 4 * n + 4, 128:256]], axis=0
                )
            start(step3(NPAIRS + 1))
        else:
            ff[...] = value
            done2.add(u)
            for n, (ua, ub) in enumerate(PAIRS):
                if u in (ua, ub) and ua in done2 and ub in done2:
                    va, vb = f2[ua], f2[ub]
                    for q in range(4):
                        s3[n, q] = jnp.concatenate([va[4 * q : 4 * q + 4], vb[4 * q : 4 * q + 4]], axis=0)
                    start(step3(n))

    red[0] = jnp.zeros((16, 128), F32)

    def end_third(n):
        if n < NPAIRS:
            src, rec, out, k = s3.at[n], rx3.at[n], fin.at[n], CLASS[PAIRS[n][0]]
        elif n == NPAIRS:
            src, rec, out, k = s3_s, rx3_s, fin_s, 2
        else:
            src, rec, out, k = s3_g, rx3_g, fin_g, 2
        for copy in step3(n):
            copy.wait_recv()
        value = src[along(ORDER[k][2])] + rec[0] + rec[1] + rec[2]
        out[...] = value
        sq = value * value
        if n < NPAIRS:
            sq = sq[:, 0:128] + sq[:, 128:256] + sq[:, 256:384] + sq[:, 384:512]
        elif n == NPAIRS:
            sq = sq[0:8] + sq[8:16]
        red[0, 8:16] = red[0, 8:16] + sq

    def put(u, a, g):
        rows = a.shape[0]
        xt[:, 0:rows] = dot_nt(order_of(CLASS[u]), a).astype(BF16)
        if u >= OUT_SLOTS:
            step0(u - OUT_SLOTS).wait_send()
        o, out_r = bufs(u)[:2]
        value = dot(xt[:, 0:rows], g)
        o[...] = value[0:256]
        out_r[...] = value[256:512]
        start([step0(u)])

    def gates(layer):
        def tile(t):
            scalar = mx[layer, 0:ATOMS, lanes(t)]
            gate = jax.nn.sigmoid(scalar)
            dy0 = dyb[0:ATOMS, lanes(t)]
            dgate = jnp.zeros((ATOMS, 128), F32)
            dskip = dy0 * xb[layer, 0:ATOMS, lanes(t)].astype(F32)
            for m in range(1, 16):
                dy = dyb[comp_rows(m), lanes(t)]
                dmx[comp_rows(m), lanes(t)] = (dy * gate).astype(BF16)
                dgate += dy * mx[layer, comp_rows(m), lanes(t)]
                dskip += dy * xb[layer, comp_rows(m), lanes(t)].astype(F32)
            slope = gate * (1.0 - gate)
            dmx[0:ATOMS, lanes(t)] = (dy0 * (gate + scalar * slope) + dgate * slope).astype(BF16)
            dsk[layer, :, lanes(t)] = dskip

        each_tile(tile)
        if layer == 1:
            pl.semaphore_wait(barrier, 22)

    def product(u):
        if u == SEC:
            second_product()
        elif u == GAIN:
            gain_product()
        else:
            which, layer, d = MATS[u]
            rows = rows_of(*LEVELS[d])
            if which == "out":
                put(u, sm[layer, rows, :], dmx[rows, :])
            else:
                put(u, xb[layer, rows, :], dl[rows, :])

    def summed_grad(layer):
        for d, (a, b) in enumerate(LEVELS):
            dsb[rows_of(a, b), :] = dot_nt(dmx[rows_of(a, b), :], wout[layer, d]) * 0.25

    def message_grad(n):
        layer, t = n // 4, n % 4
        for s in range(4):
            src0 = lg[layer, 0, edge_rows(s), lanes(t)].astype(F32)
            total0 = jnp.zeros((ATOMS, 128), F32)
            for d, (a, b) in enumerate(LEVELS):
                weight = rad[layer, edge_rows(s), lanes(t, d * C)]
                by_harm = jnp.zeros((ATOMS, 128), F32)
                by_src = jnp.zeros((ATOMS, 128), F32)
                for m in range(a, b):
                    dt = dsb[comp_rows(m), lanes(t)]
                    by_harm += abc[m, edge_rows(s), :] * dt
                    if m == 0:
                        by_src += dt * src0
                        total0 += dt * weight
                    else:
                        by_src += dt * lg[layer, m, edge_rows(s), lanes(t)].astype(F32)
                        lg[layer, m, edge_rows(s), lanes(t)] = (dt * weight).astype(BF16)
                dr[layer, edge_rows(s), lanes(t, d * C)] = (by_harm * src0 + by_src).astype(BF16)
                total0 += weight * by_harm
            lg[layer, 0, edge_rows(s), lanes(t)] = total0.astype(BF16)

    def lifted_grad(layer):
        for m in range(16):
            dl[comp_rows(m), :] = dot(scatter, lg[layer, m]).astype(BF16)

    def input_grad(layer):
        for d, (a, b) in enumerate(LEVELS):
            dsb[rows_of(a, b), :] = dot_nt(dl[rows_of(a, b), :], wup[layer, d])

        def tile(t):
            skip_gain = grow[layer, :, lanes(t)]
            for m in range(16):
                dyb[comp_rows(m), lanes(t)] = (
                    dsb[comp_rows(m), lanes(t)] + skip_gain * dyb[comp_rows(m), lanes(t)]
                )

        each_tile(tile)

    def radial_grad(_):
        term = jnp.zeros((8, 128), F32)
        for layer in (0, 1):
            dhid = dot_nt(dr[layer], wsec[layer])
            p = pre[layer]
            sg = jax.nn.sigmoid(p)
            term += dot(basis2, dhid * (sg * (1.0 + p * (1.0 - sg))), HIGH)
        red[0, 0:8] = term

    def second_product():
        for d in range(4):
            wide = slice(d * C, (d + 1) * C)
            blk = dot_tn(hid[0], dr[0, :, wide]) + dot_tn(hid[1], dr[1, :, wide])
            turn[...] = jnp.transpose(blk)
            own_s[256 * d : 256 * d + 256, :] = turn[pl.ds(pl.multiple_of(c * 256, 256), 256), :]
            outb_s[256 * d : 256 * d + 256, :] = turn[pl.ds(pl.multiple_of((1 - c) * 256, 256), 256), :]
        start([step0(SEC)])

    def gain_product():
        for layer in (0, 1):
            hi = dsk[layer].astype(BF16)
            lo = (dsk[layer] - hi.astype(F32)).astype(BF16)
            rows = dot_nt(order_of(2), jnp.concatenate([hi, lo], axis=0)).astype(BF16)
            blk = dot(rows, jnp.concatenate([kind_b, kind_b], axis=0))
            own_g[:, 128 * layer : 128 * layer + 128] = blk[0:256]
            outb_g[:, 128 * layer : 128 * layer + 128] = blk[256:512]
        start([step0(GAIN)])

    saves = []

    def feature_grad(_):
        fgb[...] = dot(picks((r & 15) * 32 + (r >> 4)), dyb[...].astype(BF16)).astype(BF16)
        saves.append(pltpu.make_async_copy(fgb, fg_o, wsem.at[6]))
        saves[0].start()

    actions = {
        "G": gates, "P": product, "S": summed_grad, "K": message_grad, "L": lifted_grad, "X": input_grad,
        "R": radial_grad, "F": feature_grad,
        "A": from_core, "B": pass_on, "C": end_first, "D": end_second, "E": end_third,
    }
    for step in STEPS:
        actions[step[0]](int(step[1:]))

    def all_sum(stage, n):
        p = lax.axis_index("inner") if stage == 0 else lax.axis_index("outer")
        base = 8 * stage

        def copy(j, slot):
            return pltpu.make_async_remote_copy(
                src_ref=red.at[stage], dst_ref=redrx.at[base + slot],
                send_sem=ssr.at[base + j], recv_sem=rsr.at[base + slot],
                device_id=group_peer(stage, j), device_id_type=MESH,
            )

        return [copy(j, p) for j in range(1, n)], [copy(j, (p + j) % n) for j in range(1, n)], base, p

    for stage, n in GROUPS:
        copies, waits, base, p = all_sum(stage, n)
        for one in copies:
            one.start()
        redrx[base + p] = red[stage]
        if stage == 0:
            for q, (src, dst) in enumerate(((fin, fin_h), (fin_s, fin_sh), (fin_g, fin_gh))):
                saves.append(pltpu.make_async_copy(src, dst, wsem.at[10 + q]))
                saves[-1].start()
            for u in range(NUNITS):
                if not (u < 16 and u + OUT_SLOTS < 16):
                    step0(u).wait_send()
                for copy in step1(u) + step2(u):
                    copy.wait_send()
            for q in range(NPAIRS + 2):
                for copy in step3(q):
                    copy.wait_send()
        for one in waits:
            one.wait_recv()
        value = redrx[base]
        for j in range(1, n):
            value = value + redrx[base + j]
        red[stage + 1] = value
    sums[...] = red[2]

    for stage, n in GROUPS:
        for copy in all_sum(stage, n)[0]:
            copy.wait_send()
    for one in saves:
        one.wait()


def finish(fin, fin_s, fin_g, sums, fg, up_o, first_o, sec_o, out_o, gain_o, fg_o):
    fg_o[...] = fg[...]
    first_sum = sums[0:8]
    total = sums[8:16] + first_sum * first_sum
    total = jnp.sum(jnp.sum(total, axis=1, keepdims=True), axis=0, keepdims=True)
    scale = jnp.minimum(1.0, CLIP_NORM / jnp.sqrt(total + 1e-6))
    for n, pair in enumerate(PAIRS):
        value = fin[n] * scale
        for half, u in enumerate(pair):
            which, layer, d = MATS[u]
            ref = up_o if which == "up" else out_o
            ref[layer, d] = value[4 * half : 4 * half + 4]
    scaled = first_sum * scale
    second = fin_s[...] * scale
    gains = fin_g[...] * scale
    for layer in (0, 1):
        first_o[layer] = scaled[:, 64 * layer : 64 * layer + 64]
        sec_o[layer] = second[:, 64 * layer : 64 * layer + 64]
        gain_o[layer] = gains[4 * layer : 4 * layer + 4, 0:89]


def per_device(features, cotangent, counts, senders, angular, basis, species, w_up, w_first, w_second, w_out, gain):
    vm, hbm = pl.BlockSpec(memory_space=pltpu.VMEM), pl.BlockSpec(memory_space=pl.ANY)
    V = pltpu.VMEM
    dma = pltpu.SemaphoreType.DMA
    scratch = [
        V((C, C), BF16), V((C, C), BF16), V((89, 2, C), F32),
        V((2, 4, C, C), BF16), V((2, 4, C, C), BF16), V((2, 128, 2048), BF16), V((2, 8, 128), F32), V((2, 128, C), F32), dma((13,)),
        V((2, C, C), BF16),
        V((2, 16, EDGES, C), BF16),
        V((2, EDGES, 2048), F32),
        V((2, EDGES, 128), F32),
        V((2, EDGES, 128), BF16),
        V((2, C, C), BF16),
        V((2, C, C), F32),
        V((2, ATOMS, C), F32),
        V((16, EDGES, 128), F32),
        V((C, C), BF16),
        V((C, C), F32),
        V((C, C), BF16),
        V((C, C), F32),
        V((2, EDGES, 2048), BF16),
        V((C, C), BF16),
        V((C, 128), F32),
        V((C, 256), BF16),
        V((3, C, C), BF16),
        V((2, ATOMS, C), F32),
        V((C, C), BF16),
        V((16, 256, C), F32), V((1024, 128), F32), V((256, 256), F32),
        V((OUT_SLOTS, 256, C), F32), V((1024, 128), F32), V((256, 256), F32),
        V((16, 256, C), F32), V((1024, 128), F32), V((256, 256), F32),
        V((16, 6, 32, C), F32), V((6, 128, 128), F32), V((6, 32, 256), F32),
        V((16, 3, 16, C), F32), V((3, 64, 128), F32), V((3, 16, 256), F32),
        V((16, 16, C), F32), V((64, 128), F32), V((16, 256), F32),
        V((NPAIRS, 4, 8, C), F32), V((4, 16, 128), F32), V((4, 8, 128), F32),
        V((NPAIRS, 3, 8, C), F32), V((3, 16, 128), F32), V((3, 8, 128), F32),
        V((NPAIRS, 8, C), F32), V((16, 128), F32), V((8, 128), F32),
        V((3, 16, 128), F32), V((24, 16, 128), F32),
        dma((NUNITS,)), dma((NUNITS,)), dma((6 * NUNITS,)), dma((6 * NUNITS,)),
        dma((3 * NUNITS,)), dma((3 * NUNITS,)), dma((3 * (NPAIRS + 2),)), dma((3 * (NPAIRS + 2),)),
        dma((24,)), dma((24,)),
    ]
    shape = jax.ShapeDtypeStruct
    sums = pl.pallas_call(
        kernel,
        name="interaction_grads",
        out_shape=(
            shape((NPAIRS, 8, C), F32), shape((16, 128), F32), shape((8, 128), F32), shape((16, 128), F32),
            shape((C, C), BF16),
        ),
        in_specs=[pl.BlockSpec(memory_space=pltpu.SMEM)] + [vm] * 5 + [hbm] * 6,
        out_specs=(hbm,) * 3 + (vm, hbm),
        scratch_shapes=scratch,
        compiler_params=pltpu.CompilerParams(
            collective_id=0, has_side_effects=True, vmem_limit_bytes=63 * 2**20
        ),
        cost_estimate=pl.CostEstimate(flops=8 * 10**9, bytes_accessed=12 * 10**6, transcendentals=10**5),
    )(
        counts, senders, angular, basis, species.reshape(1, ATOMS), w_first,
        features.reshape(C, C), cotangent.reshape(C, C), jnp.transpose(gain, (1, 0, 2)), w_up, w_second, w_out,
    )
    up, first, second, out, gain_grad, feature_grad = pl.pallas_call(
        finish,
        name="clip",
        out_shape=(
            shape((2, 4, 4, C), F32), shape((2, 8, 64), F32), shape((2, 16, 64), F32),
            shape((2, 4, 4, C), F32), shape((2, 4, 89), F32), shape((C, C), BF16),
        ),
        in_specs=[vm] * 5,
        out_specs=(vm,) * 6,
    )(*sums)
    return (
        up, first, jnp.transpose(second, (0, 2, 1)), out, jnp.transpose(gain_grad, (0, 2, 1)),
        feature_grad.reshape(features.shape),
    )


def solution(mesh):
    both = ("inner", "outer")
    return jax.shard_map(
        per_device,
        mesh=mesh,
        in_specs=(
            P(both, None, None), P(both, None, None), P(both), P(None, both), P(None, None, both),
            P(None, None, both), P(both), P(), P(), P(), P(), P(),
        ),
        out_specs=(
            P(None, None, both, None), P(), P(None, None, both), P(None, None, both, None),
            P(None, None, both), P(both, None, None),
        ),
        check_vma=False,
    )
```
